512 devices in a mesh: blk: 64 (over z_lo, y, core), grp: 8 (over z_hi, x).
Axes of the slice: x: 4, y: 8, z: 8 (z_hi: 2, z_lo: 4; z = z_hi * 4 + z_lo), core: 2. Of those that a mesh axis runs over, the one named last changes fastest.
Arguments:
- feats: bfloat16 [256, 131072], P('grp', 'blk'), may hold values from -6 to 6
- weight: bfloat16 [256, 256], replicated, may hold values from -0.375 to 0.375
- nbr: int32 [16, 131072], P('grp', 'blk'), may hold values from 0 to 131071, as said below
- mult: bfloat16 [16, 131072], P('grp', 'blk'), may hold values from 0.099609375 to 3
- cotan: bfloat16 [256, 131072], P('grp', 'blk'), may hold values from -6 to 6
Outputs:
- hidden: bfloat16 [256, 131072], P('grp', 'blk')
- grad_feats: float32 [256, 131072], P('grp', 'blk')
- grad_weight: float32 [256, 256], P('grp')
The draws below stay inside these ranges and needn't reach their ends.
Inputs may be any that keep to these rules, and one draw needn't show every extreme that they name: `nbr`: the neighbours of a node in block b of 2048 nodes lie in blocks b, b - 1, ..., b - 3, counted cyclically over the 64 blocks. A program may pack these indices, or parts of them, several to a word for any transfer; this is an exception to the 16-bit rule below.
All inputs are finite; a program needn't handle non-finite values.
Results may differ from the reference program's by a relative error of at most 0.02.
Values may be sent and summed in bfloat16 or wider, within the bound.
A program may use at most 128 MiB of HBM per device.

```python
import math
import jax
import jax.numpy as jnp
from jax import lax

F = 256
K = 16
BAND = 4
ROWS = 2048
N = 131072


def draw_nbr(key, part):
    blocks = N // ROWS
    first, second = jax.random.split(jax.random.fold_in(key, 17))
    offset = jax.random.randint(first, (K, N), 0, BAND)
    local_index = jax.random.randint(second, (K, N), 0, ROWS)
    own_block = jnp.arange(N, dtype=jnp.int32) // ROWS
    target = (own_block[None, :] - offset + blocks) % blocks
    return (target * ROWS + local_index).astype(jnp.int32)


def block_scale(own_key, extent, cuts, least, top_value):
    gain, own = 1.0, jax.random.fold_in(own_key, 6)
    for dim, shards_of in cuts:
        steps = jnp.exp(jax.random.uniform(jax.random.fold_in(own, dim), (shards_of,), jnp.float32, least / len(cuts), top_value / len(cuts)))
        gain = gain * jnp.repeat(steps, extent[dim] // shards_of).reshape([-1 if axis == dim else 1 for axis in range(len(extent))])
    return gain


def gaussian(stream_key, dims, spread, most, pieces=(), kind=jnp.bfloat16):
    values = jax.random.normal(stream_key, dims, jnp.float32) * spread
    if len(pieces) > 0:
        values = block_scale(stream_key, dims, pieces, -0.22, 0.18) * values
    return jnp.clip(values, min=-most, max=most).astype(kind)


def setup_inputs(seed: int = 0) -> dict:
    key_list = jax.random.split(jax.random.key(seed), 6)
    feats = gaussian(key_list[0], (F, N), 1.0, 6.0, ((0, 8), (1, 64)))
    weight = gaussian(key_list[1], (F, F), F ** -0.5, 0.375)
    nbr = draw_nbr(jax.random.fold_in(key_list[5], 71), 0)
    mult = jnp.clip(jnp.exp(math.log(3.0) - 3.4051113 * jax.random.uniform(key_list[3], (K, N), jnp.float32) ** block_scale(key_list[3], (K, N), ((0, 8), (1, 64)), -0.2, 0.2)), 0.099609375, 3.0).astype(jnp.bfloat16)
    cotan = gaussian(key_list[4], (F, N), 1.0, 6.0, ((0, 8), (1, 64)))
    return dict(feats=feats, weight=weight, nbr=nbr, mult=mult, cotan=cotan)


def reference(feats, weight, nbr, mult, cotan):
    edge_weight = mult.astype(jnp.float32)
    degree = 1.0 + lax.optimization_barrier(jnp.sum(edge_weight, axis=0))
    root_inv = lax.rsqrt(degree)
    scaled = (feats.astype(jnp.float32) * root_inv).astype(jnp.bfloat16)
    summed = scaled.astype(jnp.float32)
    for k in range(K):
        summed = summed + edge_weight[k] * jnp.take(scaled, nbr[k], axis=1).astype(jnp.float32)
    aggregated = (root_inv * summed).astype(jnp.bfloat16)
    z_value = jnp.dot(weight.T, aggregated, preferred_element_type=jnp.float32)
    hidden = jax.nn.silu(z_value).astype(jnp.bfloat16)
    logistic = jax.nn.sigmoid(z_value)
    grad_z = (cotan.astype(jnp.float32) * logistic * (1.0 + z_value * (1.0 - logistic))).astype(jnp.bfloat16)
    grad_weight = lax.dot_general(aggregated, grad_z, (((1,), (1,)), ((), ())), preferred_element_type=jnp.float32) * N ** (-0.5)
    grad_agg = jnp.dot(weight, grad_z, preferred_element_type=jnp.float32)
    scaled_grad = (root_inv * grad_agg).astype(jnp.bfloat16).astype(jnp.float32)
    gathered = jnp.zeros_like(scaled_grad)
    for k in range(K):
        gathered = gathered.at[:, nbr[k]].add(edge_weight[k] * scaled_grad)
    grad_feats = root_inv * (scaled_grad + gathered)
    return (hidden, grad_feats, grad_weight)
```

```python
import functools

import jax
import jax.numpy as jnp
from jax import lax
from jax.experimental import pallas as pl
from jax.experimental.pallas import tpu as pltpu
from jax.sharding import PartitionSpec as P

BAND = 4
CORES = 2
RINGS = 8
BF = jnp.bfloat16
F32 = jnp.float32
MESH = pl.DeviceIdType.MESH
NT = (((1,), (1,)), ((), ()))
WORDS, MULTS, COTS, AGGS, SGS, HIDS, GWS, RSUM, ZSUM, RALL = range(10)


def kernel(
    shape,
    feats,
    weight,
    words,
    mults,
    cotan,
    hidden,
    grad_feats,
    grad_weight,
    gw,
    gm,
    cot_all,
    halo,
    agg_own,
    agg_all,
    sg_own,
    sg,
    hid_own,
    adj,
    e_lo,
    e_hi,
    e_m,
    root,
    w_t,
    part,
    arrived,
    gw_own,
    gw_in,
    t_own,
    t_in,
    u_own,
    u_in,
    v_own,
    v_in,
    send_sem,
    recv_sem,
    hsend,
    hrecv,
):
    blocks, groups, rings = shape
    feat, rows = feats.shape
    width = feat * groups
    slice_n = rows // groups
    spans = blocks // rings
    edge_rows = words.shape[0]
    b = lax.axis_index("blk")
    g = lax.axis_index("grp")
    core = lax.rem(b, CORES)
    ring = lax.rem(b // CORES, rings)
    z_lo = b // (CORES * rings)
    span = z_lo * CORES + core

    def grp_dev(q):
        return (b, q)

    def ring_dev(q):
        return ((z_lo * rings + q) * CORES + core, g)

    def span_dev(q):
        return (((q // CORES) * rings + ring) * CORES + lax.rem(q, CORES), g)

    def rows_of(q):
        return pl.ds(pl.multiple_of(q * feat, feat), feat)

    def nodes_of(q):
        return pl.ds(pl.multiple_of(q * slice_n, slice_n), slice_n)

    def edges_of(q):
        return pl.ds(pl.multiple_of(q * edge_rows, 16), edge_rows)

    plans = {
        WORDS: (grp_dev, g, groups, lambda q: words, lambda q: gw.at[edges_of(q), :]),
        MULTS: (grp_dev, g, groups, lambda q: mults, lambda q: gm.at[:, edges_of(q), :]),
        COTS: (grp_dev, g, groups, lambda q: cotan.at[:, nodes_of(q)], lambda q: cot_all.at[rows_of(q), :]),
        AGGS: (grp_dev, g, groups, lambda q: agg_own.at[:, nodes_of(q)], lambda q: agg_all.at[rows_of(q), :]),
        SGS: (grp_dev, g, groups, lambda q: sg_own.at[rows_of(q), :], lambda q: sg.at[:, nodes_of(q)]),
        HIDS: (grp_dev, g, groups, lambda q: hid_own.at[rows_of(q), :], lambda q: hidden.at[:, nodes_of(q)]),
        GWS: (grp_dev, g, groups, lambda q: gw_own.at[rows_of(q), :], lambda q: gw_in.at[q]),
        RSUM: (ring_dev, ring, rings, lambda q: t_own.at[q], lambda q: t_in.at[q]),
        ZSUM: (span_dev, span, spans, lambda q: u_own, lambda q: u_in.at[q]),
        RALL: (ring_dev, ring, rings, lambda q: v_own, lambda q: v_in.at[q]),
    }

    def out_copy(phase, q):
        dev, me, _, src, dst = plans[phase]
        return pltpu.make_async_remote_copy(
            src_ref=src(q),
            dst_ref=dst(me),
            send_sem=send_sem.at[phase, q],
            recv_sem=recv_sem.at[phase, me],
            device_id=dev(q),
            device_id_type=MESH,
        )

    def in_copy(phase, q):
        dev, me, _, src, dst = plans[phase]
        return pltpu.make_async_remote_copy(
            src_ref=src(q),
            dst_ref=dst(q),
            send_sem=send_sem.at[phase, q],
            recv_sem=recv_sem.at[phase, q],
            device_id=dev(q),
            device_id_type=MESH,
        )

    def each(phase, act):
        me, count = plans[phase][1], plans[phase][2]

        @pl.loop(1, count)
        def _(i):
            act(lax.rem(me + i, count))

    def send_all(phase):
        each(phase, lambda q: out_copy(phase, q).start())

    def wait_all(phase):
        each(phase, lambda q: in_copy(phase, q).wait_recv())

    def sent_all(phase):
        each(phase, lambda q: out_copy(phase, q).wait_send())

    def halo_copy(off):
        return pltpu.make_async_remote_copy(
            src_ref=halo.at[:, pl.ds(0, rows)],
            dst_ref=halo.at[:, pl.ds(off * rows, rows)],
            send_sem=hsend.at[0, off - 1],
            recv_sem=hrecv.at[0, off - 1],
            device_id=(lax.rem(b + off, blocks), g),
            device_id_type=MESH,
        )

    def back_copy(off):
        return pltpu.make_async_remote_copy(
            src_ref=part.at[off - 1],
            dst_ref=arrived.at[off - 1],
            send_sem=hsend.at[1, off - 1],
            recv_sem=hrecv.at[1, off - 1],
            device_id=(lax.rem(b - off + blocks, blocks), g),
            device_id_type=MESH,
        )

    barrier = pltpu.get_barrier_semaphore()

    def greet(dev):
        pl.semaphore_signal(barrier, inc=1, device_id=dev, device_id_type=MESH)

    for phase in (WORDS, RSUM, ZSUM):
        each(phase, lambda q, dev=plans[phase][0]: greet(dev(q)))
    for off in range(1, BAND):
        greet((lax.rem(b + off, blocks), g))
        greet((lax.rem(b - off + blocks, blocks), g))
    pl.semaphore_wait(barrier, groups - 1 + rings - 1 + spans - 1 + 2 * (BAND - 1))

    send_all(WORDS)
    send_all(MULTS)
    send_all(COTS)
    gw[edges_of(g), :] = words[...]
    gm[:, edges_of(g), :] = mults[...]
    cot_all[rows_of(g), :] = cotan[:, nodes_of(g)]
    w_t[...] = weight[...].astype(F32).T.astype(BF)
    wait_all(WORDS)
    wait_all(MULTS)

    half = gw.shape[0]
    for h in range(2):
        code = (gw[...] >> (16 * h)) & 0xFFFF
        at = pl.ds(h * half, half)
        e_lo[:, at] = (code & 255).astype(F32).T
        e_hi[:, at] = (code >> 8).astype(F32).T
        e_m[:, at] = gm[h].astype(F32).T
    edges = 2 * half
    fold = (
        lax.rem(lax.broadcasted_iota(jnp.int32, (edges, 128), 0), 16)
        == lax.rem(lax.broadcasted_iota(jnp.int32, (edges, 128), 1), 16)
    )
    fold = jnp.where(fold, 1.0, 0.0).astype(BF)
    degree = jnp.dot(e_m[...].astype(BF), fold, preferred_element_type=F32)
    pick = (
        lax.broadcasted_iota(jnp.int32, (8, 128), 0)
        == lax.broadcasted_iota(jnp.int32, (8, 128), 1) // 16
    )
    for c in range(rows // 128):
        line = jnp.sum(jnp.where(pick, degree[c * 8 : c * 8 + 8, :], 0.0), axis=0, keepdims=True)
        root[:, c * 128 : c * 128 + 128] = lax.rsqrt(1.0 + line)
    halo[:, pl.ds(0, rows)] = (feats[...].astype(F32) * root[...]).astype(BF)
    for off in range(1, BAND):
        halo_copy(off).start()

    hi_count = BAND * rows // 256
    sub = lax.broadcasted_iota(jnp.int32, (16, edges), 0)
    own_lane = lax.rem(lax.broadcasted_iota(jnp.int32, (16, edges), 1), 16) == sub
    sub_f = sub.astype(F32)

    @pl.loop(0, rows // 16)
    def _(t):
        one = pl.ds(t, 1)
        low = (jnp.broadcast_to(e_lo[one, :], (16, edges)) - sub_f).astype(BF)
        high = jnp.broadcast_to(e_hi[one, :], (16, edges)).astype(BF)
        amount = jnp.where(own_lane, jnp.broadcast_to(e_m[one, :], (16, edges)), 0.0).astype(BF)
        zero = jnp.zeros((16, edges), BF)
        ones = jnp.ones((16, edges), BF)
        right = jnp.concatenate(
            [jnp.where(low == jnp.asarray(16.0 * c, BF), ones, zero) for c in range(16)], axis=0
        )
        left = jnp.concatenate(
            [jnp.where(high == jnp.asarray(float(c), BF), amount, zero) for c in range(hi_count)],
            axis=0,
        )
        made = lax.dot_general(left, right, NT, preferred_element_type=F32).astype(BF)
        adj[pl.ds(pl.multiple_of(t * 16, 16), 16), :] = jnp.concatenate(
            [made[c * 16 : c * 16 + 16, :] for c in range(hi_count)], axis=1
        )

    for off in range(1, BAND):
        halo_copy(off).wait_recv()

    step_n = 256

    def forward(q):
        @pl.loop(0, slice_n // step_n)
        def _(i):
            at = pl.ds(pl.multiple_of(q * slice_n + i * step_n, step_n), step_n)
            total = halo[:, at].astype(F32) + lax.dot_general(
                halo[...], adj[at, :], NT, preferred_element_type=F32
            )
            agg_own[:, at] = (root[:, at] * total).astype(BF)

    def forward_send(q):
        forward(q)
        out_copy(AGGS, q).start()

    each(AGGS, forward_send)
    forward(g)
    agg_all[rows_of(g), :] = agg_own[:, nodes_of(g)]
    wait_all(AGGS)
    wait_all(COTS)

    z = jnp.dot(w_t[...], agg_all[...], preferred_element_type=F32)
    s = 1.0 / (1.0 + jnp.exp(-z))
    grad_z = (cot_all[...].astype(F32) * s * (1.0 + z * (1.0 - s))).astype(BF)
    grad_agg = jnp.dot(weight[...], grad_z, preferred_element_type=F32)
    sg_own[...] = (root[:, nodes_of(g)] * grad_agg).astype(BF)
    send_all(SGS)
    gw_own[...] = lax.dot_general(agg_all[...], grad_z, NT, preferred_element_type=F32)
    send_all(GWS)
    hid_own[...] = (z * s).astype(BF)
    send_all(HIDS)
    sg[:, nodes_of(g)] = sg_own[rows_of(g), :]
    gw_in[g] = gw_own[rows_of(g), :]
    hidden[:, nodes_of(g)] = hid_own[rows_of(g), :]
    wait_all(SGS)

    chunk = feat // (rings // 2)
    for off in range(BAND - 1, -1, -1):

        @pl.loop(0, rows // 256)
        def _(i, off=off):
            at = pl.ds(pl.multiple_of(i * 256, 256), 256)
            src = pl.ds(pl.multiple_of(off * rows + i * 256, 256), 256)
            value = jnp.dot(sg[...], adj[:, src], preferred_element_type=F32)
            if off > 0:
                part[off - 1, :, at] = value.astype(BF)
            else:
                grad_feats[:, at] = value + sg[:, at].astype(F32)

        if off > 0:
            back_copy(off).start()
        if off == 3:
            wait_all(GWS)
            total = gw_in[0]
            for q in range(1, groups):
                total = total + gw_in[q]
            for q in range(rings):
                t_own[q] = total[
                    (q // 2) * chunk : (q // 2 + 1) * chunk, (q % 2) * 128 : (q % 2) * 128 + 128
                ]
            send_all(RSUM)
            t_in[ring] = t_own[ring]
        elif off == 2:
            wait_all(RSUM)
            total = t_in[0]
            for q in range(1, rings):
                total = total + t_in[q]
            u_own[...] = total
            send_all(ZSUM)
            u_in[span] = u_own[...]
        elif off == 1:
            wait_all(ZSUM)
            total = u_in[0]
            for q in range(1, spans):
                total = total + u_in[q]
            v_own[...] = total * (rows * blocks) ** (-0.5)
            send_all(RALL)
            v_in[ring] = v_own[...]

    wait_all(RALL)
    for q in range(rings):
        grad_weight[
            (q // 2) * chunk : (q // 2 + 1) * chunk, (q % 2) * 128 : (q % 2) * 128 + 128
        ] = v_in[q]
    for off in range(1, BAND):
        back_copy(off).wait_recv()
    carried = arrived[0].astype(F32)
    for off in range(2, BAND):
        carried = carried + arrived[off - 1].astype(F32)
    grad_feats[...] = root[...] * (grad_feats[...] + carried)
    wait_all(HIDS)
    for phase in plans:
        sent_all(phase)
    for off in range(1, BAND):
        halo_copy(off).wait_send()
        back_copy(off).wait_send()


def body(rings, feats, weight, nbr, mult, cotan):
    feat, rows = feats.shape
    slots = nbr.shape[0]
    blocks = lax.axis_size("blk")
    groups = lax.axis_size("grp")
    width = feat * groups
    slice_n = rows // groups
    b = lax.axis_index("blk")
    code = ((b - nbr // rows + blocks) % blocks) * rows + nbr % rows
    code = code.reshape(slots // 2, 2, rows // 16, 16)
    words = (code[:, 0] + code[:, 1] * 65536).transpose(0, 2, 1).reshape(slots * 8, rows // 16)
    mults = mult.reshape(slots // 2, 2, rows // 16, 16).transpose(1, 0, 3, 2)
    mults = mults.reshape(2, slots * 8, rows // 16)
    chunk = feat // (rings // 2)
    spans = blocks // rings
    vmem = pltpu.VMEM
    edges = 256
    most = max(groups, rings, spans)
    return tuple(
        pl.pallas_call(
            functools.partial(kernel, (blocks, groups, rings)),
            out_shape=(
                jax.ShapeDtypeStruct((feat, rows), BF),
                jax.ShapeDtypeStruct((feat, rows), F32),
                jax.ShapeDtypeStruct((feat, width), F32),
            ),
            in_specs=[pl.BlockSpec(memory_space=vmem)] * 5,
            out_specs=(pl.BlockSpec(memory_space=vmem),) * 3,
            scratch_shapes=[
                vmem((edges // 2, 128), jnp.int32),
                vmem((2, edges // 2, 128), BF),
                vmem((width, slice_n), BF),
                vmem((feat, BAND * rows), BF),
                vmem((feat, rows), BF),
                vmem((width, slice_n), BF),
                vmem((width, slice_n), BF),
                vmem((feat, rows), BF),
                vmem((width, slice_n), BF),
                vmem((rows, BAND * rows), BF),
                vmem((128, edges), F32),
                vmem((128, edges), F32),
                vmem((128, edges), F32),
                vmem((1, rows), F32),
                vmem((width, width), BF),
                vmem((BAND - 1, feat, rows), BF),
                vmem((BAND - 1, feat, rows), BF),
                vmem((width, width), F32),
                vmem((groups, feat, width), F32),
                vmem((rings, chunk, 128), F32),
                vmem((rings, chunk, 128), F32),
                vmem((chunk, 128), F32),
                vmem((spans, chunk, 128), F32),
                vmem((chunk, 128), F32),
                vmem((rings, chunk, 128), F32),
                pltpu.SemaphoreType.DMA((10, most)),
                pltpu.SemaphoreType.DMA((10, most)),
                pltpu.SemaphoreType.DMA((2, BAND - 1)),
                pltpu.SemaphoreType.DMA((2, BAND - 1)),
            ],
            compiler_params=pltpu.CompilerParams(
                collective_id=0, has_side_effects=True, vmem_limit_bytes=56 * 1024 * 1024
            ),
        )(feats, weight, words, mults, cotan)
    )


def solution(mesh, rings=RINGS):
    return jax.shard_map(
        functools.partial(body, rings),
        mesh=mesh,
        in_specs=(P("grp", "blk"), P(), P("grp", "blk"), P("grp", "blk"), P("grp", "blk")),
        out_specs=(P("grp", "blk"), P("grp", "blk"), P("grp", None)),
        check_vma=False,
    )
```

```python
import functools

import jax
import jax.numpy as jnp
from jax import lax
from jax.experimental import pallas as pl
from jax.experimental.pallas import tpu as pltpu
from jax.sharding import PartitionSpec as P

BAND = 4
CORES = 2
RINGS = 8
BF = jnp.bfloat16
F32 = jnp.float32
MESH = pl.DeviceIdType.MESH
NT = (((1,), (1,)), ((), ()))
WORDS, MULTS, COTS, AGGS, SGS, HIDS, XSUM, RSUM, ZSUM, RALL = range(10)
ZHI = 2
PLANE = 16
HI = 16


def kernel(
    shape,
    feats,
    weight,
    nbr,
    mult,
    cotan,
    hidden,
    grad_feats,
    grad_weight,
    words,
    mults,
    gw,
    gm,
    cot_all,
    halo,
    agg_own,
    agg_all,
    sg_own,
    sg,
    hid_own,
    adj,
    spread,
    e_lq,
    e_lr,
    e_hi,
    e_m,
    root,
    w_t,
    part,
    arrived,
    gw_own,
    gw_in,
    t_own,
    t_in,
    u_own,
    u_in,
    v_own,
    v_in,
    send_sem,
    recv_sem,
    hsend,
    hrecv,
):
    blocks, groups, rings = shape
    feat, rows = feats.shape
    width = feat * groups
    slice_n = rows // groups
    spans = blocks // rings
    edge_rows = words.shape[0]
    b = lax.axis_index("blk")
    g = lax.axis_index("grp")
    core = lax.rem(b, CORES)
    ring = lax.rem(b // CORES, rings)
    z_lo = b // (CORES * rings)
    xs = groups // ZHI
    z_hi = g // xs
    x = lax.rem(g, xs)
    span = (z_hi * spans + z_lo * CORES + core)

    def grp_dev(q):
        return (b, q)

    def ring_dev(q):
        return ((z_lo * rings + q) * CORES + core, g)

    def x_dev(q):
        return (b, z_hi * xs + q)

    def span_dev(q):
        low = lax.rem(q, spans)
        return (
            ((low // CORES) * rings + ring) * CORES + lax.rem(low, CORES),
            (q // spans) * xs + x,
        )

    def rows_of(q):
        return pl.ds(pl.multiple_of(q * feat, feat), feat)

    def nodes_of(q):
        return pl.ds(pl.multiple_of(q * slice_n, slice_n), slice_n)

    def edges_of(q):
        return pl.ds(pl.multiple_of(q * edge_rows, 16), edge_rows)

    plans = {
        WORDS: (grp_dev, g, groups, lambda q: words, lambda q: gw.at[edges_of(q), :]),
        MULTS: (grp_dev, g, groups, lambda q: mults, lambda q: gm.at[:, edges_of(q), :]),
        COTS: (grp_dev, g, groups, lambda q: cotan.at[:, nodes_of(q)], lambda q: cot_all.at[rows_of(q), :]),
        AGGS: (grp_dev, g, groups, lambda q: agg_own.at[:, nodes_of(q)], lambda q: agg_all.at[rows_of(q), :]),
        SGS: (grp_dev, g, groups, lambda q: sg_own.at[rows_of(q), :], lambda q: sg.at[:, nodes_of(q)]),
        HIDS: (grp_dev, g, groups, lambda q: hid_own.at[rows_of(q), :], lambda q: hidden.at[:, nodes_of(q)]),
        XSUM: (x_dev, x, xs, lambda q: gw_own.at[:, q], lambda q: gw_in.at[q]),
        RSUM: (ring_dev, ring, rings, lambda q: t_own.at[q], lambda q: t_in.at[q]),
        ZSUM: (span_dev, span, ZHI * spans, lambda q: u_own.at[q // spans], lambda q: u_in.at[q]),
        RALL: (ring_dev, ring, rings, lambda q: v_own, lambda q: v_in.at[q]),
    }

    def out_copy(phase, q):
        dev, me, _, src, dst = plans[phase]
        return pltpu.make_async_remote_copy(
            src_ref=src(q),
            dst_ref=dst(me),
            send_sem=send_sem.at[phase, q],
            recv_sem=recv_sem.at[phase, me],
            device_id=dev(q),
            device_id_type=MESH,
        )

    def in_copy(phase, q):
        dev, me, _, src, dst = plans[phase]
        return pltpu.make_async_remote_copy(
            src_ref=src(q),
            dst_ref=dst(q),
            send_sem=send_sem.at[phase, q],
            recv_sem=recv_sem.at[phase, q],
            device_id=dev(q),
            device_id_type=MESH,
        )

    def each(phase, act):
        me, count = plans[phase][1], plans[phase][2]

        @pl.loop(1, count)
        def _(i):
            act(lax.rem(me + i, count))

    def send_all(phase):
        each(phase, lambda q: out_copy(phase, q).start())

    def wait_all(phase):
        each(phase, lambda q: in_copy(phase, q).wait_recv())

    def sent_all(phase):
        each(phase, lambda q: out_copy(phase, q).wait_send())

    def halo_copy(off):
        return pltpu.make_async_remote_copy(
            src_ref=halo.at[:, pl.ds(0, rows)],
            dst_ref=halo.at[:, pl.ds(off * rows, rows)],
            send_sem=hsend.at[0, off - 1],
            recv_sem=hrecv.at[0, off - 1],
            device_id=(lax.rem(b + off, blocks), g),
            device_id_type=MESH,
        )

    def back_copy(off):
        return pltpu.make_async_remote_copy(
            src_ref=part.at[off - 1],
            dst_ref=arrived.at[off - 1],
            send_sem=hsend.at[1, off - 1],
            recv_sem=hrecv.at[1, off - 1],
            device_id=(lax.rem(b - off + blocks, blocks), g),
            device_id_type=MESH,
        )

    barrier = pltpu.get_barrier_semaphore()

    def greet(dev):
        pl.semaphore_signal(barrier, inc=1, device_id=dev, device_id_type=MESH)

    for phase in (WORDS, RSUM, ZSUM):
        each(phase, lambda q, dev=plans[phase][0]: greet(dev(q)))
    for off in range(1, BAND):
        greet((lax.rem(b + off, blocks), g))
        greet((lax.rem(b - off + blocks, blocks), g))

    pairs = nbr.shape[0] // 2
    shift = rows.bit_length() - 1
    code = nbr[...]
    code = (((b - (code >> shift)) & (blocks - 1)) << shift) + (code & (rows - 1))
    amounts = mult[...].astype(F32)

    def plane(value, k):
        return jnp.concatenate(
            [value[k : k + 1, c * 128 : c * 128 + 128] for c in range(PLANE)], axis=0
        )

    for p in range(pairs):
        at = pl.ds(p * PLANE, PLANE)
        words[at, :] = plane(code, 2 * p) + (plane(code, 2 * p + 1) << 16)
        for h in range(2):
            mults[h, at, :] = plane(amounts, 2 * p + h).astype(BF)
    pl.semaphore_wait(
        barrier, groups - 1 + rings - 1 + ZHI * spans - 1 + 2 * (BAND - 1)
    )

    send_all(WORDS)
    send_all(MULTS)
    gw[edges_of(g), :] = words[...]
    gm[:, edges_of(g), :] = mults[...]
    cot_all[rows_of(g), :] = cotan[:, nodes_of(g)]
    w_t[...] = weight[...].astype(F32).T.astype(BF)
    edges = 256
    lane_e = lax.broadcasted_iota(jnp.int32, (128, edges), 1)
    row_l = lax.broadcasted_iota(jnp.int32, (128, edges), 0)
    folds = (lane_e & 15) == (row_l & 15)
    for k in range(16):
        spread[k * 128 : k * 128 + 128, :] = jnp.where(
            folds & ((lane_e >> 4) == k), 1.0, 0.0
        ).astype(BF)
    wait_all(MULTS)

    planes = gw.shape[0] // PLANE
    line = jnp.zeros((PLANE, 128), F32)
    for h in range(2):
        for q in range(planes):
            line = line + gm[h, q * PLANE : q * PLANE + PLANE, :].astype(F32)
    line = lax.rsqrt(1.0 + line)
    for c in range(PLANE):
        root[:, c * 128 : c * 128 + 128] = line[c : c + 1, :]
    halo[:, pl.ds(0, rows)] = (feats[...].astype(F32) * root[...]).astype(BF)
    for off in range(1, BAND):
        halo_copy(off).start()
    send_all(COTS)
    wait_all(WORDS)

    seat = (
        lax.broadcasted_iota(jnp.int32, (PLANE, 8, 128), 2) >> 4
    ) == lax.broadcasted_iota(jnp.int32, (PLANE, 8, 128), 1)

    def seated(value):
        wide = jnp.broadcast_to(value.astype(F32)[:, None, :], (PLANE, 8, 128))
        return jnp.where(seat, wide, 0.0).reshape(PLANE * 8, 128).astype(BF)

    def table(pick):
        wide = jnp.concatenate(
            [seated(pick(h, pl.ds(q * PLANE, PLANE))) for h in range(2) for q in range(planes)],
            axis=1,
        )
        return jnp.dot(wide, spread[...], preferred_element_type=F32)

    def field(low, mask):
        return lambda h, at: (gw[at, :] >> (16 * h + low)) & mask

    e_lr[...] = table(field(0, 15))
    e_lq[...] = table(field(4, 31))
    e_hi[...] = table(field(9, 15))
    e_m[...] = table(lambda h, at: gm[h, at, :])

    lo_chunks = BAND * rows // HI // 16
    sub = lax.broadcasted_iota(jnp.int32, (16, edges), 0)
    own_lane = (lax.broadcasted_iota(jnp.int32, (16, edges), 1) & 15) == sub
    sub_f = sub.astype(F32)
    zero = jnp.zeros((16, edges), BF)
    ones = jnp.ones((16, edges), BF)

    @pl.loop(0, rows // 16, unroll=8)
    def _(t):
        one = pl.ds(t, 1)

        def row(ref):
            return jnp.broadcast_to(ref[one, :], (16, edges))

        low = jnp.where(row(e_lr) == sub_f, row(e_lq), -1.0).astype(BF)
        high = row(e_hi).astype(BF)
        amount = jnp.where(own_lane, row(e_m), 0.0).astype(BF)
        right = jnp.concatenate(
            [jnp.where(low == jnp.asarray(float(c), BF), ones, zero) for c in range(lo_chunks)],
            axis=0,
        )
        left = jnp.concatenate(
            [jnp.where(high == jnp.asarray(float(c), BF), amount, zero) for c in range(HI)],
            axis=0,
        )
        made = lax.dot_general(left, right, NT, preferred_element_type=F32).astype(BF)
        adj[pl.ds(pl.multiple_of(t * 16, 16), 16), :] = jnp.concatenate(
            [made[c * 16 : c * 16 + 16, :] for c in range(HI)], axis=1
        )

    for off in range(1, BAND):
        halo_copy(off).wait_recv()

    step_n = 256

    def forward(q):
        @pl.loop(0, slice_n // step_n)
        def _(i):
            at = pl.ds(pl.multiple_of(q * slice_n + i * step_n, step_n), step_n)
            total = halo[:, at].astype(F32) + lax.dot_general(
                halo[...], adj[at, :], NT, preferred_element_type=F32
            )
            agg_own[:, at] = (root[:, at] * total).astype(BF)

    def forward_send(q):
        forward(q)
        out_copy(AGGS, q).start()

    each(AGGS, forward_send)
    forward(g)
    agg_all[rows_of(g), :] = agg_own[:, nodes_of(g)]
    wait_all(AGGS)
    wait_all(COTS)

    z = jnp.dot(w_t[...], agg_all[...], preferred_element_type=F32)
    s = 1.0 / (1.0 + jnp.exp(-z))
    grad_z = (cot_all[...].astype(F32) * s * (1.0 + z * (1.0 - s))).astype(BF)
    grad_agg = jnp.dot(weight[...], grad_z, preferred_element_type=F32)
    sg_own[...] = (root[:, nodes_of(g)] * grad_agg).astype(BF)
    send_all(SGS)
    product = lax.dot_general(agg_all[...], grad_z, NT, preferred_element_type=F32)
    for q in range(groups):
        gw_own[q // xs, q % xs] = product[q * feat : q * feat + feat, :]
    send_all(XSUM)
    hid_own[...] = (z * s).astype(BF)
    send_all(HIDS)
    sg[:, nodes_of(g)] = sg_own[rows_of(g), :]
    gw_in[x] = gw_own[:, x]
    hidden[:, nodes_of(g)] = hid_own[rows_of(g), :]
    wait_all(SGS)

    chunk = feat // (rings // 2)
    for off in range(BAND - 1, -1, -1):

        @pl.loop(0, rows // 256)
        def _(i, off=off):
            at = pl.ds(pl.multiple_of(i * 256, 256), 256)
            src = pl.ds(pl.multiple_of(off * rows + i * 256, 256), 256)
            value = jnp.dot(sg[...], adj[:, src], preferred_element_type=F32)
            if off > 0:
                part[off - 1, :, at] = value.astype(BF)
            else:
                grad_feats[:, at] = value + sg[:, at].astype(F32)

        if off > 0:
            back_copy(off).start()
        if off == 3:
            wait_all(XSUM)
            total = gw_in[0]
            for q in range(1, xs):
                total = total + gw_in[q]
            for q in range(rings):
                t_own[q] = total[
                    :, (q // 2) * chunk : (q // 2 + 1) * chunk, (q % 2) * 128 : (q % 2) * 128 + 128
                ]
            send_all(RSUM)
            t_in[ring] = t_own[ring]
        elif off == 2:
            wait_all(RSUM)
            total = t_in[0]
            for q in range(1, rings):
                total = total + t_in[q]
            u_own[...] = total
            send_all(ZSUM)
            u_in[span] = u_own[z_hi]
        elif off == 1:
            wait_all(ZSUM)
            total = u_in[0]
            for q in range(1, ZHI * spans):
                total = total + u_in[q]
            v_own[...] = total * (rows * blocks) ** (-0.5)
            send_all(RALL)
            v_in[ring] = v_own[...]

    wait_all(RALL)
    for q in range(rings):
        grad_weight[
            (q // 2) * chunk : (q // 2 + 1) * chunk, (q % 2) * 128 : (q % 2) * 128 + 128
        ] = v_in[q]
    for off in range(1, BAND):
        back_copy(off).wait_recv()
    carried = arrived[0].astype(F32)
    for off in range(2, BAND):
        carried = carried + arrived[off - 1].astype(F32)
    grad_feats[...] = root[...] * (grad_feats[...] + carried)
    wait_all(HIDS)
    for phase in plans:
        sent_all(phase)
    for off in range(1, BAND):
        halo_copy(off).wait_send()
        back_copy(off).wait_send()


def settle(*refs):
    sems = refs[6]
    copies = [pltpu.make_async_copy(refs[i], refs[3 + i], sems.at[i]) for i in range(3)]
    for copy in copies:
        copy.start()
    for copy in copies:
        copy.wait()


def body(rings, feats, weight, nbr, mult, cotan):
    feat, rows = feats.shape
    slots = nbr.shape[0]
    blocks = lax.axis_size("blk")
    groups = lax.axis_size("grp")
    width = feat * groups
    slice_n = rows // groups
    chunk = feat // (rings // 2)
    spans = blocks // rings
    vmem = pltpu.VMEM
    edges = 256
    most = max(groups, rings, ZHI * spans)
    outs = pl.pallas_call(
            functools.partial(kernel, (blocks, groups, rings)),
            out_shape=(
                jax.ShapeDtypeStruct((feat, rows), BF),
                jax.ShapeDtypeStruct((feat, rows), F32),
                jax.ShapeDtypeStruct((feat, width), F32),
            ),
            in_specs=[pl.BlockSpec(memory_space=vmem)] * 5,
            out_specs=(pl.BlockSpec(memory_space=vmem),) * 3,
            scratch_shapes=[
                vmem((slots * 8, 128), jnp.int32),
                vmem((2, slots * 8, 128), BF),
                vmem((edges // 2, 128), jnp.int32),
                vmem((2, edges // 2, 128), BF),
                vmem((width, slice_n), BF),
                vmem((feat, BAND * rows), BF),
                vmem((feat, rows), BF),
                vmem((width, slice_n), BF),
                vmem((width, slice_n), BF),
                vmem((feat, rows), BF),
                vmem((width, slice_n), BF),
                vmem((rows, BAND * rows), BF),
                vmem((16 * 128, edges), BF),
                vmem((128, edges), F32),
                vmem((128, edges), F32),
                vmem((128, edges), F32),
                vmem((128, edges), F32),
                vmem((1, rows), F32),
                vmem((width, width), BF),
                vmem((BAND - 1, feat, rows), BF),
                vmem((BAND - 1, feat, rows), BF),
                vmem((ZHI, groups // ZHI, feat, width), F32),
                vmem((groups // ZHI, ZHI, feat, width), F32),
                vmem((rings, ZHI, chunk, 128), F32),
                vmem((rings, ZHI, chunk, 128), F32),
                vmem((ZHI, chunk, 128), F32),
                vmem((ZHI * spans, chunk, 128), F32),
                vmem((chunk, 128), F32),
                vmem((rings, chunk, 128), F32),
                pltpu.SemaphoreType.DMA((10, most)),
                pltpu.SemaphoreType.DMA((10, most)),
                pltpu.SemaphoreType.DMA((2, BAND - 1)),
                pltpu.SemaphoreType.DMA((2, BAND - 1)),
            ],
            compiler_params=pltpu.CompilerParams(
                collective_id=0, has_side_effects=True, vmem_limit_bytes=46 * 1024 * 1024
            ),
        )(feats, weight, nbr, mult, cotan)
    return tuple(
        pl.pallas_call(
            settle,
            out_shape=[jax.ShapeDtypeStruct(o.shape, o.dtype) for o in outs],
            in_specs=[pl.BlockSpec(memory_space=pl.ANY)] * 3,
            out_specs=[pl.BlockSpec(memory_space=pl.ANY)] * 3,
            scratch_shapes=[pltpu.SemaphoreType.DMA((3,))],
        )(*outs)
    )


def solution(mesh, rings=RINGS):
    return jax.shard_map(
        functools.partial(body, rings),
        mesh=mesh,
        in_specs=(P("grp", "blk"), P(), P("grp", "blk"), P("grp", "blk"), P("grp", "blk")),
        out_specs=(P("grp", "blk"), P("grp", "blk"), P("grp", None)),
        check_vma=False,
    )
```

```python
import functools

import jax
import jax.numpy as jnp
from jax import lax
from jax.experimental import pallas as pl
from jax.experimental.pallas import tpu as pltpu
from jax.sharding import PartitionSpec as P

BAND = 4
CORES = 2
RINGS = 8
BF = jnp.bfloat16
F32 = jnp.float32
MESH = pl.DeviceIdType.MESH
NT = (((1,), (1,)), ((), ()))
WORDS, MULTS, COTS, AGGS, SGS, HIDS, XSUM, RSUM, ZSUM, RALL = range(10)
ZHI = 2
PLANE = 16
HI = 16


def kernel(
    shape,
    feats_in,
    weight_in,
    nbr,
    mult,
    cotan_in,
    hidden,
    grad_feats,
    grad_weight,
    words,
    mults,
    gw,
    gm,
    cot_all,
    halo,
    agg_own,
    agg_all,
    sg_own,
    sg,
    hid_own,
    adj,
    spread,
    e_lq,
    e_lr,
    e_hi,
    e_m,
    root,
    w_t,
    part,
    arrived,
    gw_own,
    gw_in,
    t_own,
    t_in,
    u_own,
    u_in,
    v_own,
    v_in,
    send_sem,
    recv_sem,
    hsend,
    hrecv,
    feats,
    weight,
    cotan,
    load_sem,
):
    blocks, groups, rings = shape
    feat, rows = feats.shape
    width = feat * groups
    slice_n = rows // groups
    spans = blocks // rings
    edge_rows = words.shape[0]
    b = lax.axis_index("blk")
    g = lax.axis_index("grp")
    core = lax.rem(b, CORES)
    ring = lax.rem(b // CORES, rings)
    z_lo = b // (CORES * rings)
    xs = groups // ZHI
    z_hi = g // xs
    x = lax.rem(g, xs)
    span = (z_hi * spans + z_lo * CORES + core)

    def grp_dev(q):
        return (b, q)

    def ring_dev(q):
        return ((z_lo * rings + q) * CORES + core, g)

    def x_dev(q):
        return (b, z_hi * xs + q)

    def span_dev(q):
        low = lax.rem(q, spans)
        return (
            ((low // CORES) * rings + ring) * CORES + lax.rem(low, CORES),
            (q // spans) * xs + x,
        )

    def rows_of(q):
        return pl.ds(pl.multiple_of(q * feat, feat), feat)

    def nodes_of(q):
        return pl.ds(pl.multiple_of(q * slice_n, slice_n), slice_n)

    def edges_of(q):
        return pl.ds(pl.multiple_of(q * edge_rows, 16), edge_rows)

    plans = {
        WORDS: (grp_dev, g, groups, lambda q: words, lambda q: gw.at[edges_of(q), :]),
        MULTS: (grp_dev, g, groups, lambda q: mults, lambda q: gm.at[:, edges_of(q), :]),
        COTS: (grp_dev, g, groups, lambda q: cotan.at[:, nodes_of(q)], lambda q: cot_all.at[rows_of(q), :]),
        AGGS: (grp_dev, g, groups, lambda q: agg_own.at[:, nodes_of(q)], lambda q: agg_all.at[rows_of(q), :]),
        SGS: (grp_dev, g, groups, lambda q: sg_own.at[rows_of(q), :], lambda q: sg.at[:, nodes_of(q)]),
        HIDS: (grp_dev, g, groups, lambda q: hid_own.at[rows_of(q), :], lambda q: hidden.at[:, nodes_of(q)]),
        XSUM: (x_dev, x, xs, lambda q: gw_own.at[:, q], lambda q: gw_in.at[q]),
        RSUM: (ring_dev, ring, rings, lambda q: t_own.at[q], lambda q: t_in.at[q]),
        ZSUM: (span_dev, span, ZHI * spans, lambda q: u_own.at[q // spans], lambda q: u_in.at[q]),
        RALL: (ring_dev, ring, rings, lambda q: v_own, lambda q: v_in.at[q]),
    }

    def out_copy(phase, q):
        dev, me, _, src, dst = plans[phase]
        return pltpu.make_async_remote_copy(
            src_ref=src(q),
            dst_ref=dst(me),
            send_sem=send_sem.at[phase, q],
            recv_sem=recv_sem.at[phase, me],
            device_id=dev(q),
            device_id_type=MESH,
        )

    def in_copy(phase, q):
        dev, me, _, src, dst = plans[phase]
        return pltpu.make_async_remote_copy(
            src_ref=src(q),
            dst_ref=dst(q),
            send_sem=send_sem.at[phase, q],
            recv_sem=recv_sem.at[phase, q],
            device_id=dev(q),
            device_id_type=MESH,
        )

    def each(phase, act):
        me, count = plans[phase][1], plans[phase][2]

        @pl.loop(1, count)
        def _(i):
            act(lax.rem(me + i, count))

    def send_all(phase):
        each(phase, lambda q: out_copy(phase, q).start())

    def wait_all(phase):
        each(phase, lambda q: in_copy(phase, q).wait_recv())

    def sent_all(phase):
        each(phase, lambda q: out_copy(phase, q).wait_send())

    def halo_copy(off):
        return pltpu.make_async_remote_copy(
            src_ref=halo.at[:, pl.ds(0, rows)],
            dst_ref=halo.at[:, pl.ds(off * rows, rows)],
            send_sem=hsend.at[0, off - 1],
            recv_sem=hrecv.at[0, off - 1],
            device_id=(lax.rem(b + off, blocks), g),
            device_id_type=MESH,
        )

    def back_copy(off):
        return pltpu.make_async_remote_copy(
            src_ref=part.at[off - 1],
            dst_ref=arrived.at[off - 1],
            send_sem=hsend.at[1, off - 1],
            recv_sem=hrecv.at[1, off - 1],
            device_id=(lax.rem(b - off + blocks, blocks), g),
            device_id_type=MESH,
        )

    loads = [
        pltpu.make_async_copy(here, there, load_sem.at[i])
        for i, (here, there) in enumerate(
            ((feats_in, feats), (weight_in, weight), (cotan_in, cotan))
        )
    ]
    for load in loads:
        load.start()
    barrier = pltpu.get_barrier_semaphore()

    def greet(dev):
        pl.semaphore_signal(barrier, inc=1, device_id=dev, device_id_type=MESH)

    for phase in (WORDS, RSUM, ZSUM):
        each(phase, lambda q, dev=plans[phase][0]: greet(dev(q)))
    for off in range(1, BAND):
        greet((lax.rem(b + off, blocks), g))
        greet((lax.rem(b - off + blocks, blocks), g))

    pairs = nbr.shape[0] // 2
    shift = rows.bit_length() - 1
    code = nbr[...]
    code = (((b - (code >> shift)) & (blocks - 1)) << shift) + (code & (rows - 1))
    amounts = mult[...].astype(F32)

    def plane(value, k):
        return jnp.concatenate(
            [value[k : k + 1, c * 128 : c * 128 + 128] for c in range(PLANE)], axis=0
        )

    for p in range(pairs):
        at = pl.ds(p * PLANE, PLANE)
        words[at, :] = plane(code, 2 * p) + (plane(code, 2 * p + 1) << 16)
        for h in range(2):
            mults[h, at, :] = plane(amounts, 2 * p + h).astype(BF)
    for load in loads:
        load.wait()
    pl.semaphore_wait(
        barrier, groups - 1 + rings - 1 + ZHI * spans - 1 + 2 * (BAND - 1)
    )

    send_all(WORDS)
    send_all(MULTS)
    gw[edges_of(g), :] = words[...]
    gm[:, edges_of(g), :] = mults[...]
    cot_all[rows_of(g), :] = cotan[:, nodes_of(g)]
    w_t[...] = weight[...].astype(F32).T.astype(BF)
    edges = 256
    lane_e = lax.broadcasted_iota(jnp.int32, (128, edges), 1)
    row_l = lax.broadcasted_iota(jnp.int32, (128, edges), 0)
    folds = (lane_e & 15) == (row_l & 15)
    for k in range(16):
        spread[k * 128 : k * 128 + 128, :] = jnp.where(
            folds & ((lane_e >> 4) == k), 1.0, 0.0
        ).astype(BF)
    wait_all(MULTS)

    planes = gw.shape[0] // PLANE
    line = jnp.zeros((PLANE, 128), F32)
    for h in range(2):
        for q in range(planes):
            line = line + gm[h, q * PLANE : q * PLANE + PLANE, :].astype(F32)
    line = lax.rsqrt(1.0 + line)
    for c in range(PLANE):
        root[:, c * 128 : c * 128 + 128] = line[c : c + 1, :]
    halo[:, pl.ds(0, rows)] = (feats[...].astype(F32) * root[...]).astype(BF)
    for off in range(1, BAND):
        halo_copy(off).start()
    send_all(COTS)
    wait_all(WORDS)

    seat = (
        lax.broadcasted_iota(jnp.int32, (PLANE, 8, 128), 2) >> 4
    ) == lax.broadcasted_iota(jnp.int32, (PLANE, 8, 128), 1)

    def seated(value):
        wide = jnp.broadcast_to(value.astype(F32)[:, None, :], (PLANE, 8, 128))
        return jnp.where(seat, wide, 0.0).reshape(PLANE * 8, 128).astype(BF)

    def table(pick):
        wide = jnp.concatenate(
            [seated(pick(h, pl.ds(q * PLANE, PLANE))) for h in range(2) for q in range(planes)],
            axis=1,
        )
        return jnp.dot(wide, spread[...], preferred_element_type=F32)

    def field(low, mask):
        return lambda h, at: (gw[at, :] >> (16 * h + low)) & mask

    e_lr[...] = table(field(0, 15))
    e_lq[...] = table(field(4, 31))
    e_hi[...] = table(field(9, 15))
    e_m[...] = table(lambda h, at: gm[h, at, :])

    lo_chunks = BAND * rows // HI // 16
    sub = lax.broadcasted_iota(jnp.int32, (16, edges), 0)
    own_lane = (lax.broadcasted_iota(jnp.int32, (16, edges), 1) & 15) == sub
    sub_f = sub.astype(F32)
    zero = jnp.zeros((16, edges), BF)
    ones = jnp.ones((16, edges), BF)

    @pl.loop(0, rows // 16, unroll=8)
    def _(t):
        one = pl.ds(t, 1)

        def row(ref):
            return jnp.broadcast_to(ref[one, :], (16, edges))

        low = jnp.where(row(e_lr) == sub_f, row(e_lq), -1.0).astype(BF)
        high = row(e_hi).astype(BF)
        amount = jnp.where(own_lane, row(e_m), 0.0).astype(BF)
        right = jnp.concatenate(
            [jnp.where(low == jnp.asarray(float(c), BF), ones, zero) for c in range(lo_chunks)],
            axis=0,
        )
        left = jnp.concatenate(
            [jnp.where(high == jnp.asarray(float(c), BF), amount, zero) for c in range(HI)],
            axis=0,
        )
        made = lax.dot_general(left, right, NT, preferred_element_type=F32).astype(BF)
        adj[pl.ds(pl.multiple_of(t * 16, 16), 16), :] = jnp.concatenate(
            [made[c * 16 : c * 16 + 16, :] for c in range(HI)], axis=1
        )

    for off in range(1, BAND):
        halo_copy(off).wait_recv()

    step_n = 256

    def forward(q):
        @pl.loop(0, slice_n // step_n)
        def _(i):
            at = pl.ds(pl.multiple_of(q * slice_n + i * step_n, step_n), step_n)
            total = halo[:, at].astype(F32) + lax.dot_general(
                halo[...], adj[at, :], NT, preferred_element_type=F32
            )
            agg_own[:, at] = (root[:, at] * total).astype(BF)

    def forward_send(q):
        forward(q)
        out_copy(AGGS, q).start()

    each(AGGS, forward_send)
    forward(g)
    agg_all[rows_of(g), :] = agg_own[:, nodes_of(g)]
    wait_all(AGGS)
    wait_all(COTS)

    z = jnp.dot(w_t[...], agg_all[...], preferred_element_type=F32)
    s = 1.0 / (1.0 + jnp.exp(-z))
    grad_z = (cot_all[...].astype(F32) * s * (1.0 + z * (1.0 - s))).astype(BF)
    grad_agg = jnp.dot(weight[...], grad_z, preferred_element_type=F32)
    sg_own[...] = (root[:, nodes_of(g)] * grad_agg).astype(BF)
    send_all(SGS)
    product = lax.dot_general(agg_all[...], grad_z, NT, preferred_element_type=F32)
    for q in range(groups):
        gw_own[q // xs, q % xs] = product[q * feat : q * feat + feat, :].astype(BF)
    send_all(XSUM)
    hid_own[...] = (z * s).astype(BF)
    sg[:, nodes_of(g)] = sg_own[rows_of(g), :]
    gw_in[x] = gw_own[:, x]
    hidden[:, nodes_of(g)] = hid_own[rows_of(g), :]

    chunk = feat // (rings // 2)
    wait_all(XSUM)
    total = gw_in[0].astype(F32)
    for q in range(1, xs):
        total = total + gw_in[q].astype(F32)
    for q in range(rings):
        t_own[q] = total[
            :, (q // 2) * chunk : (q // 2 + 1) * chunk, (q % 2) * 128 : (q % 2) * 128 + 128
        ]
    send_all(RSUM)
    t_in[ring] = t_own[ring]
    send_all(HIDS)
    wait_all(SGS)

    for off in range(BAND - 1, -1, -1):

        value = jnp.dot(
            sg[...], adj[:, pl.ds(off * rows, rows)], preferred_element_type=F32
        )
        if off > 0:
            part[off - 1] = value.astype(BF)
        else:
            grad_feats[...] = value + sg[...].astype(F32)

        if off > 0:
            back_copy(off).start()
        if off == 2:
            wait_all(RSUM)
            total = t_in[0]
            for q in range(1, rings):
                total = total + t_in[q]
            u_own[...] = total
            send_all(ZSUM)
            u_in[span] = u_own[z_hi]

    wait_all(ZSUM)
    total = u_in[0]
    for q in range(1, ZHI * spans):
        total = total + u_in[q]
    v_own[...] = total * (rows * blocks) ** (-0.5)
    send_all(RALL)
    v_in[ring] = v_own[...]
    for off in range(1, BAND):
        back_copy(off).wait_recv()
    carried = arrived[0].astype(F32)
    for off in range(2, BAND):
        carried = carried + arrived[off - 1].astype(F32)
    grad_feats[...] = root[...] * (grad_feats[...] + carried)
    wait_all(HIDS)
    wait_all(RALL)
    for q in range(rings):
        grad_weight[
            (q // 2) * chunk : (q // 2 + 1) * chunk, (q % 2) * 128 : (q % 2) * 128 + 128
        ] = v_in[q]
    for phase in plans:
        sent_all(phase)
    for off in range(1, BAND):
        halo_copy(off).wait_send()
        back_copy(off).wait_send()


def settle(*refs):
    kept, sems = refs[6:9], refs[9]
    arrive = [pltpu.make_async_copy(refs[i], kept[i], sems.at[0, i]) for i in range(3)]
    leave = [pltpu.make_async_copy(kept[i], refs[3 + i], sems.at[1, i]) for i in range(3)]
    for copy in arrive:
        copy.start()
    for i in (2, 0, 1):
        arrive[i].wait()
        leave[i].start()
    for copy in leave:
        copy.wait()


def body(rings, feats, weight, nbr, mult, cotan):
    feat, rows = feats.shape
    slots = nbr.shape[0]
    blocks = lax.axis_size("blk")
    groups = lax.axis_size("grp")
    width = feat * groups
    slice_n = rows // groups
    chunk = feat // (rings // 2)
    spans = blocks // rings
    vmem = pltpu.VMEM
    edges = 256
    most = max(groups, rings, ZHI * spans)
    outs = pl.pallas_call(
            functools.partial(kernel, (blocks, groups, rings)),
            out_shape=(
                jax.ShapeDtypeStruct((feat, rows), BF),
                jax.ShapeDtypeStruct((feat, rows), F32),
                jax.ShapeDtypeStruct((feat, width), F32),
            ),
            in_specs=[
                pl.BlockSpec(memory_space=pl.ANY if i in (0, 1, 4) else vmem) for i in range(5)
            ],
            out_specs=(pl.BlockSpec(memory_space=vmem),) * 3,
            scratch_shapes=[
                vmem((slots * 8, 128), jnp.int32),
                vmem((2, slots * 8, 128), BF),
                vmem((edges // 2, 128), jnp.int32),
                vmem((2, edges // 2, 128), BF),
                vmem((width, slice_n), BF),
                vmem((feat, BAND * rows), BF),
                vmem((feat, rows), BF),
                vmem((width, slice_n), BF),
                vmem((width, slice_n), BF),
                vmem((feat, rows), BF),
                vmem((width, slice_n), BF),
                vmem((rows, BAND * rows), BF),
                vmem((16 * 128, edges), BF),
                vmem((128, edges), F32),
                vmem((128, edges), F32),
                vmem((128, edges), F32),
                vmem((128, edges), F32),
                vmem((1, rows), F32),
                vmem((width, width), BF),
                vmem((BAND - 1, feat, rows), BF),
                vmem((BAND - 1, feat, rows), BF),
                vmem((ZHI, groups // ZHI, feat, width), BF),
                vmem((groups // ZHI, ZHI, feat, width), BF),
                vmem((rings, ZHI, chunk, 128), F32),
                vmem((rings, ZHI, chunk, 128), F32),
                vmem((ZHI, chunk, 128), F32),
                vmem((ZHI * spans, chunk, 128), F32),
                vmem((chunk, 128), F32),
                vmem((rings, chunk, 128), F32),
                pltpu.SemaphoreType.DMA((10, most)),
                pltpu.SemaphoreType.DMA((10, most)),
                pltpu.SemaphoreType.DMA((2, BAND - 1)),
                pltpu.SemaphoreType.DMA((2, BAND - 1)),
                vmem((feat, rows), BF),
                vmem((width, width), BF),
                vmem((feat, rows), BF),
                pltpu.SemaphoreType.DMA((3,)),
            ],
            compiler_params=pltpu.CompilerParams(
                collective_id=0, has_side_effects=True, vmem_limit_bytes=60 * 1024 * 1024
            ),
        )(feats, weight, nbr, mult, cotan)
    return tuple(
        pl.pallas_call(
            settle,
            out_shape=[jax.ShapeDtypeStruct(o.shape, o.dtype) for o in outs],
            in_specs=[pl.BlockSpec(memory_space=pl.ANY)] * 3,
            out_specs=[pl.BlockSpec(memory_space=pl.ANY)] * 3,
            scratch_shapes=[pltpu.VMEM(o.shape, o.dtype) for o in outs]
            + [pltpu.SemaphoreType.DMA((2, 3))],
            compiler_params=pltpu.CompilerParams(vmem_limit_bytes=60 * 1024 * 1024),
        )(*outs)
    )


def solution(mesh, rings=RINGS):
    return jax.shard_map(
        functools.partial(body, rings),
        mesh=mesh,
        in_specs=(P("grp", "blk"), P(), P("grp", "blk"), P("grp", "blk"), P("grp", "blk")),
        out_specs=(P("grp", "blk"), P("grp", "blk"), P("grp", None)),
        check_vma=False,
    )
```

```python
import functools

import jax
import jax.numpy as jnp
from jax import lax
from jax.experimental import pallas as pl
from jax.experimental.pallas import tpu as pltpu
from jax.sharding import PartitionSpec as P

BAND = 4
CORES = 2
RINGS = 8
BF = jnp.bfloat16
F32 = jnp.float32
MESH = pl.DeviceIdType.MESH
NT = (((1,), (1,)), ((), ()))
WORDS, MULTS, COTS, AGGS, SGS, HIDS, RSUM, ZSUM, RALL = range(9)
ZHI = 2
PLANE = 16
HI = 16


def kernel(
    shape,
    feats_in,
    weight_in,
    nbr,
    mult,
    cotan_in,
    hidden,
    grad_feats,
    grad_weight,
    words,
    mults,
    gw,
    gm,
    cot_all,
    halo,
    agg_own,
    agg_all,
    sg_own,
    sg,
    hid_own,
    adj,
    spread,
    e_lq,
    e_lr,
    e_hi,
    e_m,
    root,
    w_t,
    part,
    arrived,
    t_own,
    t_in,
    u_own,
    u_in,
    v_own,
    v_in,
    send_sem,
    recv_sem,
    hsend,
    hrecv,
    feats,
    weight,
    cotan,
    load_sem,
):
    blocks, groups, rings = shape
    feat, rows = feats.shape
    width = feat * groups
    slice_n = rows // groups
    spans = blocks // rings
    edge_rows = words.shape[0]
    b = lax.axis_index("blk")
    g = lax.axis_index("grp")
    core = lax.rem(b, CORES)
    ring = lax.rem(b // CORES, rings)
    z_lo = b // (CORES * rings)
    xs = groups // ZHI
    z_hi = g // xs
    x = lax.rem(g, xs)
    span = (z_hi * spans + z_lo * CORES + core)

    def grp_dev(q):
        return (b, q)

    def ring_dev(q):
        return ((z_lo * rings + q) * CORES + core, g)

    def plane_dev(q):
        return (
            (z_lo * rings + lax.rem(q, rings)) * CORES + core,
            z_hi * xs + q // rings,
        )

    def span_dev(q):
        low = lax.rem(q, spans)
        return (
            ((low // CORES) * rings + ring) * CORES + lax.rem(low, CORES),
            (q // spans) * xs + x,
        )

    def rows_of(q):
        return pl.ds(pl.multiple_of(q * feat, feat), feat)

    def nodes_of(q):
        return pl.ds(pl.multiple_of(q * slice_n, slice_n), slice_n)

    def edges_of(q):
        return pl.ds(pl.multiple_of(q * edge_rows, 16), edge_rows)

    plans = {
        WORDS: (grp_dev, g, groups, lambda q: words, lambda q: gw.at[edges_of(q), :]),
        MULTS: (grp_dev, g, groups, lambda q: mults, lambda q: gm.at[:, edges_of(q), :]),
        COTS: (grp_dev, g, groups, lambda q: cotan.at[:, nodes_of(q)], lambda q: cot_all.at[rows_of(q), :]),
        AGGS: (grp_dev, g, groups, lambda q: agg_own.at[:, nodes_of(q)], lambda q: agg_all.at[rows_of(q), :]),
        SGS: (grp_dev, g, groups, lambda q: sg_own.at[rows_of(q), :], lambda q: sg.at[:, nodes_of(q)]),
        HIDS: (grp_dev, g, groups, lambda q: hid_own.at[rows_of(q), :], lambda q: hidden.at[:, nodes_of(q)]),
        RSUM: (plane_dev, x * rings + ring, xs * rings, lambda q: t_own.at[q], lambda q: t_in.at[q]),
        ZSUM: (span_dev, span, ZHI * spans, lambda q: u_own.at[q // spans], lambda q: u_in.at[q]),
        RALL: (ring_dev, ring, rings, lambda q: v_own, lambda q: v_in.at[q]),
    }

    def out_copy(phase, q):
        dev, me, _, src, dst = plans[phase]
        return pltpu.make_async_remote_copy(
            src_ref=src(q),
            dst_ref=dst(me),
            send_sem=send_sem.at[phase, q],
            recv_sem=recv_sem.at[phase, me],
            device_id=dev(q),
            device_id_type=MESH,
        )

    def in_copy(phase, q):
        dev, me, _, src, dst = plans[phase]
        return pltpu.make_async_remote_copy(
            src_ref=src(q),
            dst_ref=dst(q),
            send_sem=send_sem.at[phase, q],
            recv_sem=recv_sem.at[phase, q],
            device_id=dev(q),
            device_id_type=MESH,
        )

    def each(phase, act):
        me, count = plans[phase][1], plans[phase][2]

        @pl.loop(1, count)
        def _(i):
            act(lax.rem(me + i, count))

    def send_all(phase):
        each(phase, lambda q: out_copy(phase, q).start())

    def wait_all(phase):
        each(phase, lambda q: in_copy(phase, q).wait_recv())

    def sent_all(phase):
        each(phase, lambda q: out_copy(phase, q).wait_send())

    def halo_copy(off):
        return pltpu.make_async_remote_copy(
            src_ref=halo.at[:, pl.ds(0, rows)],
            dst_ref=halo.at[:, pl.ds(off * rows, rows)],
            send_sem=hsend.at[0, off - 1],
            recv_sem=hrecv.at[0, off - 1],
            device_id=(lax.rem(b + off, blocks), g),
            device_id_type=MESH,
        )

    def back_copy(off):
        return pltpu.make_async_remote_copy(
            src_ref=part.at[off - 1],
            dst_ref=arrived.at[off - 1],
            send_sem=hsend.at[1, off - 1],
            recv_sem=hrecv.at[1, off - 1],
            device_id=(lax.rem(b - off + blocks, blocks), g),
            device_id_type=MESH,
        )

    loads = [
        pltpu.make_async_copy(here, there, load_sem.at[i])
        for i, (here, there) in enumerate(
            ((feats_in, feats), (weight_in, weight), (cotan_in, cotan))
        )
    ]
    for load in loads:
        load.start()
    barrier = pltpu.get_barrier_semaphore()

    def greet(dev):
        pl.semaphore_signal(barrier, inc=1, device_id=dev, device_id_type=MESH)

    for phase in (WORDS, RSUM, ZSUM):
        each(phase, lambda q, dev=plans[phase][0]: greet(dev(q)))
    for off in range(1, BAND):
        greet((lax.rem(b + off, blocks), g))
        greet((lax.rem(b - off + blocks, blocks), g))

    pairs = nbr.shape[0] // 2
    shift = rows.bit_length() - 1
    code = nbr[...]
    code = (((b - (code >> shift)) & (blocks - 1)) << shift) + (code & (rows - 1))
    amounts = mult[...].astype(F32)

    def plane(value, k):
        return jnp.concatenate(
            [value[k : k + 1, c * 128 : c * 128 + 128] for c in range(PLANE)], axis=0
        )

    for p in range(pairs):
        at = pl.ds(p * PLANE, PLANE)
        words[at, :] = plane(code, 2 * p) + (plane(code, 2 * p + 1) << 16)
        for h in range(2):
            mults[h, at, :] = plane(amounts, 2 * p + h).astype(BF)
    for load in loads:
        load.wait()
    pl.semaphore_wait(
        barrier, groups - 1 + xs * rings - 1 + ZHI * spans - 1 + 2 * (BAND - 1)
    )

    send_all(WORDS)
    send_all(MULTS)
    gw[edges_of(g), :] = words[...]
    gm[:, edges_of(g), :] = mults[...]
    cot_all[rows_of(g), :] = cotan[:, nodes_of(g)]
    w_t[...] = weight[...].astype(F32).T.astype(BF)
    edges = 256
    lane_e = lax.broadcasted_iota(jnp.int32, (128, edges), 1)
    row_l = lax.broadcasted_iota(jnp.int32, (128, edges), 0)
    folds = (lane_e & 15) == (row_l & 15)
    for k in range(16):
        spread[k * 128 : k * 128 + 128, :] = jnp.where(
            folds & ((lane_e >> 4) == k), 1.0, 0.0
        ).astype(BF)
    wait_all(MULTS)

    planes = gw.shape[0] // PLANE
    line = jnp.zeros((PLANE, 128), F32)
    for h in range(2):
        for q in range(planes):
            line = line + gm[h, q * PLANE : q * PLANE + PLANE, :].astype(F32)
    line = lax.rsqrt(1.0 + line)
    for c in range(PLANE):
        root[:, c * 128 : c * 128 + 128] = line[c : c + 1, :]
    halo[:, pl.ds(0, rows)] = (feats[...].astype(F32) * root[...]).astype(BF)
    for off in range(1, BAND):
        halo_copy(off).start()
    send_all(COTS)
    wait_all(WORDS)

    seat = (
        lax.broadcasted_iota(jnp.int32, (PLANE, 8, 128), 2) >> 4
    ) == lax.broadcasted_iota(jnp.int32, (PLANE, 8, 128), 1)

    def seated(value):
        wide = jnp.broadcast_to(value.astype(F32)[:, None, :], (PLANE, 8, 128))
        return jnp.where(seat, wide, 0.0).reshape(PLANE * 8, 128).astype(BF)

    def table(pick):
        wide = jnp.concatenate(
            [seated(pick(h, pl.ds(q * PLANE, PLANE))) for h in range(2) for q in range(planes)],
            axis=1,
        )
        return jnp.dot(wide, spread[...], preferred_element_type=F32)

    def field(low, mask):
        return lambda h, at: (gw[at, :] >> (16 * h + low)) & mask

    e_lr[...] = table(field(0, 15))
    e_lq[...] = table(field(4, 31))
    e_hi[...] = table(field(9, 15))
    e_m[...] = table(lambda h, at: gm[h, at, :])

    lo_chunks = BAND * rows // HI // 16
    sub = lax.broadcasted_iota(jnp.int32, (16, edges), 0)
    own_lane = (lax.broadcasted_iota(jnp.int32, (16, edges), 1) & 15) == sub
    sub_f = sub.astype(F32)
    zero = jnp.zeros((16, edges), BF)
    ones = jnp.ones((16, edges), BF)

    @pl.loop(0, rows // 16, unroll=32)
    def _(t):
        one = pl.ds(t, 1)

        def row(ref):
            return jnp.broadcast_to(ref[one, :], (16, edges))

        low = jnp.where(row(e_lr) == sub_f, row(e_lq), -1.0).astype(BF)
        high = row(e_hi).astype(BF)
        amount = jnp.where(own_lane, row(e_m), 0.0).astype(BF)
        right = jnp.concatenate(
            [jnp.where(low == jnp.asarray(float(c), BF), ones, zero) for c in range(lo_chunks)],
            axis=0,
        )
        left = jnp.concatenate(
            [jnp.where(high == jnp.asarray(float(c), BF), amount, zero) for c in range(HI)],
            axis=0,
        )
        made = lax.dot_general(left, right, NT, preferred_element_type=F32).astype(BF)
        adj[pl.ds(pl.multiple_of(t * 16, 16), 16), :] = jnp.concatenate(
            [made[c * 16 : c * 16 + 16, :] for c in range(HI)], axis=1
        )

    for off in range(1, BAND):
        halo_copy(off).wait_recv()

    step_n = 256

    def forward(q):
        @pl.loop(0, slice_n // step_n)
        def _(i):
            at = pl.ds(pl.multiple_of(q * slice_n + i * step_n, step_n), step_n)
            total = halo[:, at].astype(F32) + lax.dot_general(
                halo[...], adj[at, :], NT, preferred_element_type=F32
            )
            agg_own[:, at] = (root[:, at] * total).astype(BF)

    def forward_send(q):
        forward(q)
        out_copy(AGGS, q).start()

    each(AGGS, forward_send)
    forward(g)
    agg_all[rows_of(g), :] = agg_own[:, nodes_of(g)]
    wait_all(AGGS)
    wait_all(COTS)

    z = jnp.dot(w_t[...], agg_all[...], preferred_element_type=F32)
    s = 1.0 / (1.0 + jnp.exp(-z))
    grad_z = (cot_all[...].astype(F32) * s * (1.0 + z * (1.0 - s))).astype(BF)
    grad_agg = jnp.dot(weight[...], grad_z, preferred_element_type=F32)
    sg_own[...] = (root[:, nodes_of(g)] * grad_agg).astype(BF)
    send_all(SGS)
    product = lax.dot_general(agg_all[...], grad_z, NT, preferred_element_type=F32)
    chunk = feat // (rings // 2)
    for q in range(xs * rings):
        for h in range(ZHI):
            top = (h * xs + q // rings) * feat + (q % rings // 2) * chunk
            t_own[q, h * chunk : h * chunk + chunk, :] = product[
                top : top + chunk, (q % 2) * 128 : (q % 2) * 128 + 128
            ].astype(BF)
    send_all(RSUM)
    t_in[x * rings + ring] = t_own[x * rings + ring]
    hid_own[...] = (z * s).astype(BF)
    sg[:, nodes_of(g)] = sg_own[rows_of(g), :]
    hidden[:, nodes_of(g)] = hid_own[rows_of(g), :]

    send_all(HIDS)
    wait_all(SGS)

    for off in range(BAND - 1, -1, -1):

        value = jnp.dot(
            sg[...], adj[:, pl.ds(off * rows, rows)], preferred_element_type=F32
        )
        if off > 0:
            part[off - 1] = value.astype(BF)
        else:
            grad_feats[...] = value + sg[...].astype(F32)

        if off > 0:
            back_copy(off).start()
        if off == 3:
            wait_all(RSUM)
            total = t_in[0].astype(F32)
            for q in range(1, xs * rings):
                total = total + t_in[q].astype(F32)
            for h in range(ZHI):
                u_own[h] = total[h * chunk : h * chunk + chunk]
            send_all(ZSUM)
            u_in[span] = u_own[z_hi]

    wait_all(ZSUM)
    total = u_in[0]
    for q in range(1, ZHI * spans):
        total = total + u_in[q]
    v_own[...] = total * (rows * blocks) ** (-0.5)
    send_all(RALL)
    v_in[ring] = v_own[...]
    for off in range(1, BAND):
        back_copy(off).wait_recv()
    carried = arrived[0].astype(F32)
    for off in range(2, BAND):
        carried = carried + arrived[off - 1].astype(F32)
    grad_feats[...] = root[...] * (grad_feats[...] + carried)
    wait_all(HIDS)
    wait_all(RALL)
    for q in range(rings):
        grad_weight[
            (q // 2) * chunk : (q // 2 + 1) * chunk, (q % 2) * 128 : (q % 2) * 128 + 128
        ] = v_in[q]
    for phase in plans:
        sent_all(phase)
    for off in range(1, BAND):
        halo_copy(off).wait_send()
        back_copy(off).wait_send()


def settle(*refs):
    kept, sems = refs[6:9], refs[9]
    arrive = [pltpu.make_async_copy(refs[i], kept[i], sems.at[0, i]) for i in range(3)]
    leave = [pltpu.make_async_copy(kept[i], refs[3 + i], sems.at[1, i]) for i in range(3)]
    for copy in arrive:
        copy.start()
    for i in (2, 0, 1):
        arrive[i].wait()
        leave[i].start()
    for copy in leave:
        copy.wait()


def body(rings, feats, weight, nbr, mult, cotan):
    feat, rows = feats.shape
    slots = nbr.shape[0]
    blocks = lax.axis_size("blk")
    groups = lax.axis_size("grp")
    width = feat * groups
    slice_n = rows // groups
    chunk = feat // (rings // 2)
    spans = blocks // rings
    vmem = pltpu.VMEM
    edges = 256
    most = max(groups, rings * groups // ZHI, ZHI * spans)
    outs = pl.pallas_call(
            functools.partial(kernel, (blocks, groups, rings)),
            out_shape=(
                jax.ShapeDtypeStruct((feat, rows), BF),
                jax.ShapeDtypeStruct((feat, rows), F32),
                jax.ShapeDtypeStruct((feat, width), F32),
            ),
            in_specs=[
                pl.BlockSpec(memory_space=pl.ANY if i in (0, 1, 4) else vmem) for i in range(5)
            ],
            out_specs=(pl.BlockSpec(memory_space=vmem),) * 3,
            scratch_shapes=[
                vmem((slots * 8, 128), jnp.int32),
                vmem((2, slots * 8, 128), BF),
                vmem((edges // 2, 128), jnp.int32),
                vmem((2, edges // 2, 128), BF),
                vmem((width, slice_n), BF),
                vmem((feat, BAND * rows), BF),
                vmem((feat, rows), BF),
                vmem((width, slice_n), BF),
                vmem((width, slice_n), BF),
                vmem((feat, rows), BF),
                vmem((width, slice_n), BF),
                vmem((rows, BAND * rows), BF),
                vmem((16 * 128, edges), BF),
                vmem((128, edges), F32),
                vmem((128, edges), F32),
                vmem((128, edges), F32),
                vmem((128, edges), F32),
                vmem((1, rows), F32),
                vmem((width, width), BF),
                vmem((BAND - 1, feat, rows), BF),
                vmem((BAND - 1, feat, rows), BF),
                vmem((rings * groups // ZHI, ZHI * chunk, 128), BF),
                vmem((rings * groups // ZHI, ZHI * chunk, 128), BF),
                vmem((ZHI, chunk, 128), F32),
                vmem((ZHI * spans, chunk, 128), F32),
                vmem((chunk, 128), F32),
                vmem((rings, chunk, 128), F32),
                pltpu.SemaphoreType.DMA((9, most)),
                pltpu.SemaphoreType.DMA((9, most)),
                pltpu.SemaphoreType.DMA((2, BAND - 1)),
                pltpu.SemaphoreType.DMA((2, BAND - 1)),
                vmem((feat, rows), BF),
                vmem((width, width), BF),
                vmem((feat, rows), BF),
                pltpu.SemaphoreType.DMA((3,)),
            ],
            compiler_params=pltpu.CompilerParams(
                collective_id=0, has_side_effects=True, vmem_limit_bytes=60 * 1024 * 1024
            ),
        )(feats, weight, nbr, mult, cotan)
    return tuple(
        pl.pallas_call(
            settle,
            out_shape=[jax.ShapeDtypeStruct(o.shape, o.dtype) for o in outs],
            in_specs=[pl.BlockSpec(memory_space=pl.ANY)] * 3,
            out_specs=[pl.BlockSpec(memory_space=pl.ANY)] * 3,
            scratch_shapes=[pltpu.VMEM(o.shape, o.dtype) for o in outs]
            + [pltpu.SemaphoreType.DMA((2, 3))],
            compiler_params=pltpu.CompilerParams(vmem_limit_bytes=60 * 1024 * 1024),
        )(*outs)
    )


def solution(mesh, rings=RINGS):
    return jax.shard_map(
        functools.partial(body, rings),
        mesh=mesh,
        in_specs=(P("grp", "blk"), P(), P("grp", "blk"), P("grp", "blk"), P("grp", "blk")),
        out_specs=(P("grp", "blk"), P("grp", "blk"), P("grp", None)),
        check_vma=False,
    )
```

```python
import functools

import jax
import jax.numpy as jnp
from jax import lax
from jax.experimental import pallas as pl
from jax.experimental.pallas import tpu as pltpu
from jax.sharding import PartitionSpec as P

BAND = 4
CORES = 2
RINGS = 8
BF = jnp.bfloat16
F32 = jnp.float32
MESH = pl.DeviceIdType.MESH
NT = (((1,), (1,)), ((), ()))
WORDS, MULTS, COTS, AGGS, SGS, HIDS, RSUM, ZSUM, RALL = range(9)
ZHI = 2
PLANE = 16
HI = 16


def kernel(
    shape,
    feats_in,
    weight_in,
    nbr,
    mult,
    cotan_in,
    hidden,
    grad_feats,
    grad_weight,
    words,
    mults,
    gw,
    gm,
    cot_all,
    halo,
    agg_own,
    agg_all,
    sg_own,
    sg,
    hid_own,
    adj,
    spread,
    e_lq,
    e_lr,
    e_hi,
    e_m,
    root,
    w_t,
    part,
    arrived,
    t_own,
    t_in,
    u_own,
    u_in,
    v_own,
    v_in,
    send_sem,
    recv_sem,
    hsend,
    hrecv,
    feats,
    weight,
    cotan,
    load_sem,
):
    blocks, groups, rings = shape
    feat, rows = feats.shape
    width = feat * groups
    slice_n = rows // groups
    spans = blocks // rings
    edge_rows = words.shape[0]
    b = lax.axis_index("blk")
    g = lax.axis_index("grp")
    core = lax.rem(b, CORES)
    ring = lax.rem(b // CORES, rings)
    z_lo = b // (CORES * rings)
    xs = groups // ZHI
    z_hi = g // xs
    x = lax.rem(g, xs)
    span = (z_hi * spans + z_lo * CORES + core)

    def grp_dev(q):
        return (b, q)

    def ring_dev(q):
        return ((z_lo * rings + q) * CORES + core, g)

    def plane_dev(q):
        return (
            (z_lo * rings + lax.rem(q, rings)) * CORES + core,
            z_hi * xs + q // rings,
        )

    def span_dev(q):
        low = lax.rem(q, spans)
        return (
            ((low // CORES) * rings + ring) * CORES + lax.rem(low, CORES),
            (q // spans) * xs + x,
        )

    def rows_of(q):
        return pl.ds(pl.multiple_of(q * feat, feat), feat)

    def nodes_of(q):
        return pl.ds(pl.multiple_of(q * slice_n, slice_n), slice_n)

    def edges_of(q):
        return pl.ds(pl.multiple_of(q * edge_rows, 16), edge_rows)

    plans = {
        WORDS: (grp_dev, g, groups, lambda q: words, lambda q: gw.at[edges_of(q), :]),
        MULTS: (grp_dev, g, groups, lambda q: mults, lambda q: gm.at[:, edges_of(q), :]),
        COTS: (grp_dev, g, groups, lambda q: cotan.at[:, nodes_of(q)], lambda q: cot_all.at[rows_of(q), :]),
        AGGS: (grp_dev, g, groups, lambda q: agg_own.at[:, nodes_of(q)], lambda q: agg_all.at[rows_of(q), :]),
        SGS: (grp_dev, g, groups, lambda q: sg_own.at[rows_of(q), :], lambda q: sg.at[:, nodes_of(q)]),
        HIDS: (grp_dev, g, groups, lambda q: hid_own.at[rows_of(q), :], lambda q: hidden.at[:, nodes_of(q)]),
        RSUM: (plane_dev, x * rings + ring, xs * rings, lambda q: t_own.at[q], lambda q: t_in.at[q]),
        ZSUM: (span_dev, span, ZHI * spans, lambda q: u_own.at[q // spans], lambda q: u_in.at[q]),
        RALL: (ring_dev, ring, rings, lambda q: v_own, lambda q: v_in.at[q]),
    }

    def out_copy(phase, q):
        dev, me, _, src, dst = plans[phase]
        return pltpu.make_async_remote_copy(
            src_ref=src(q),
            dst_ref=dst(me),
            send_sem=send_sem.at[phase, q],
            recv_sem=recv_sem.at[phase, me],
            device_id=dev(q),
            device_id_type=MESH,
        )

    def in_copy(phase, q):
        dev, me, _, src, dst = plans[phase]
        return pltpu.make_async_remote_copy(
            src_ref=src(q),
            dst_ref=dst(q),
            send_sem=send_sem.at[phase, q],
            recv_sem=recv_sem.at[phase, q],
            device_id=dev(q),
            device_id_type=MESH,
        )

    def each(phase, act):
        me, count = plans[phase][1], plans[phase][2]

        @pl.loop(1, count)
        def _(i):
            act(lax.rem(me + i, count))

    def send_all(phase):
        each(phase, lambda q: out_copy(phase, q).start())

    def wait_all(phase):
        each(phase, lambda q: in_copy(phase, q).wait_recv())

    def sent_all(phase):
        each(phase, lambda q: out_copy(phase, q).wait_send())

    def halo_copy(off):
        return pltpu.make_async_remote_copy(
            src_ref=halo.at[:, pl.ds(0, rows)],
            dst_ref=halo.at[:, pl.ds(off * rows, rows)],
            send_sem=hsend.at[0, off - 1],
            recv_sem=hrecv.at[0, off - 1],
            device_id=(lax.rem(b + off, blocks), g),
            device_id_type=MESH,
        )

    def back_copy(off):
        return pltpu.make_async_remote_copy(
            src_ref=part.at[off - 1],
            dst_ref=arrived.at[off - 1],
            send_sem=hsend.at[1, off - 1],
            recv_sem=hrecv.at[1, off - 1],
            device_id=(lax.rem(b - off + blocks, blocks), g),
            device_id_type=MESH,
        )

    loads = [
        pltpu.make_async_copy(here, there, load_sem.at[i])
        for i, (here, there) in enumerate(
            ((feats_in, feats), (weight_in, weight), (cotan_in, cotan))
        )
    ]
    for load in loads:
        load.start()
    barrier = pltpu.get_barrier_semaphore()

    def greet(dev):
        pl.semaphore_signal(barrier, inc=1, device_id=dev, device_id_type=MESH)

    for phase in (WORDS, RSUM, ZSUM):
        each(phase, lambda q, dev=plans[phase][0]: greet(dev(q)))
    for off in range(1, BAND):
        greet((lax.rem(b + off, blocks), g))
        greet((lax.rem(b - off + blocks, blocks), g))

    pairs = nbr.shape[0] // 2
    shift = rows.bit_length() - 1
    code = nbr[...]
    code = (((b - (code >> shift)) & (blocks - 1)) << shift) + (code & (rows - 1))
    amounts = mult[...].astype(F32)

    def plane(value, k):
        return jnp.concatenate(
            [value[k : k + 1, c * 128 : c * 128 + 128] for c in range(PLANE)], axis=0
        )

    for p in range(pairs):
        at = pl.ds(p * PLANE, PLANE)
        words[at, :] = plane(code, 2 * p) + (plane(code, 2 * p + 1) << 16)
        for h in range(2):
            mults[h, at, :] = plane(amounts, 2 * p + h).astype(BF)
    for load in loads:
        load.wait()
    pl.semaphore_wait(
        barrier, groups - 1 + xs * rings - 1 + ZHI * spans - 1 + 2 * (BAND - 1)
    )

    send_all(WORDS)
    send_all(MULTS)
    gw[edges_of(g), :] = words[...]
    gm[:, edges_of(g), :] = mults[...]
    cot_all[rows_of(g), :] = cotan[:, nodes_of(g)]
    w_t[...] = weight[...].astype(F32).T.astype(BF)
    edges = 256
    lane_e = lax.broadcasted_iota(jnp.int32, (128, edges), 1)
    row_l = lax.broadcasted_iota(jnp.int32, (128, edges), 0)
    folds = (lane_e & 15) == (row_l & 15)
    for k in range(16):
        spread[k * 128 : k * 128 + 128, :] = jnp.where(
            folds & ((lane_e >> 4) == k), 1.0, 0.0
        ).astype(BF)
    wait_all(MULTS)

    planes = gw.shape[0] // PLANE
    line = jnp.zeros((PLANE, 128), F32)
    for h in range(2):
        for q in range(planes):
            line = line + gm[h, q * PLANE : q * PLANE + PLANE, :].astype(F32)
    line = lax.rsqrt(1.0 + line)
    for c in range(PLANE):
        root[:, c * 128 : c * 128 + 128] = line[c : c + 1, :]
    halo[:, pl.ds(0, rows)] = (feats[...].astype(F32) * root[...]).astype(BF)
    for off in range(1, BAND):
        halo_copy(off).start()
    send_all(COTS)
    wait_all(WORDS)

    seat = (
        lax.broadcasted_iota(jnp.int32, (PLANE, 8, 128), 2) >> 4
    ) == lax.broadcasted_iota(jnp.int32, (PLANE, 8, 128), 1)

    def seated(value):
        wide = jnp.broadcast_to(value.astype(F32)[:, None, :], (PLANE, 8, 128))
        return jnp.where(seat, wide, 0.0).reshape(PLANE * 8, 128).astype(BF)

    def table(pick):
        wide = jnp.concatenate(
            [seated(pick(h, pl.ds(q * PLANE, PLANE))) for h in range(2) for q in range(planes)],
            axis=1,
        )
        return jnp.dot(wide, spread[...], preferred_element_type=F32)

    def field(low, mask):
        return lambda h, at: (gw[at, :] >> (16 * h + low)) & mask

    e_lr[...] = table(field(0, 15))
    e_lq[...] = table(field(4, 31))
    e_hi[...] = table(field(9, 15))
    e_m[...] = table(lambda h, at: gm[h, at, :])

    lo_chunks = BAND * rows // HI // 16
    sub = lax.broadcasted_iota(jnp.int32, (16, edges), 0)
    own_lane = (lax.broadcasted_iota(jnp.int32, (16, edges), 1) & 15) == sub
    sub_f = sub.astype(F32)
    zero = jnp.zeros((16, edges), BF)
    ones = jnp.ones((16, edges), BF)

    @pl.loop(0, rows // 16, unroll=8)
    def _(t):
        one = pl.ds(t, 1)

        def row(ref):
            return jnp.broadcast_to(ref[one, :], (16, edges))

        low = jnp.where(row(e_lr) == sub_f, row(e_lq), -1.0).astype(BF)
        high = row(e_hi).astype(BF)
        amount = jnp.where(own_lane, row(e_m), 0.0).astype(BF)
        right = jnp.concatenate(
            [jnp.where(low == jnp.asarray(float(c), BF), ones, zero) for c in range(lo_chunks)],
            axis=0,
        )
        left = jnp.concatenate(
            [jnp.where(high == jnp.asarray(float(c), BF), amount, zero) for c in range(HI)],
            axis=0,
        )
        made = lax.dot_general(left, right, NT, preferred_element_type=F32).astype(BF)
        adj[pl.ds(pl.multiple_of(t * 16, 16), 16), :] = jnp.concatenate(
            [made[c * 16 : c * 16 + 16, :] for c in range(HI)], axis=1
        )

    for off in range(1, BAND):
        halo_copy(off).wait_recv()

    step_n = 256

    def forward(q):
        @pl.loop(0, slice_n // step_n)
        def _(i):
            at = pl.ds(pl.multiple_of(q * slice_n + i * step_n, step_n), step_n)
            total = halo[:, at].astype(F32) + lax.dot_general(
                halo[...], adj[at, :], NT, preferred_element_type=F32
            )
            agg_own[:, at] = (root[:, at] * total).astype(BF)

    def forward_send(q):
        forward(q)
        out_copy(AGGS, q).start()

    each(AGGS, forward_send)
    forward(g)
    agg_all[rows_of(g), :] = agg_own[:, nodes_of(g)]
    wait_all(AGGS)
    wait_all(COTS)

    z = jnp.dot(w_t[...], agg_all[...], preferred_element_type=F32)
    s = 1.0 / (1.0 + jnp.exp(-z))
    grad_z = (cot_all[...].astype(F32) * s * (1.0 + z * (1.0 - s))).astype(BF)
    product = lax.dot_general(agg_all[...], grad_z, NT, preferred_element_type=F32)
    chunk = feat // (rings // 2)
    for q in range(xs * rings):
        for h in range(ZHI):
            top = (h * xs + q // rings) * feat + (q % rings // 2) * chunk
            t_own[q, h * chunk : h * chunk + chunk, :] = product[
                top : top + chunk, (q % 2) * 128 : (q % 2) * 128 + 128
            ].astype(BF)
    send_all(RSUM)
    grad_agg = jnp.dot(weight[...], grad_z, preferred_element_type=F32)
    sg_own[...] = (root[:, nodes_of(g)] * grad_agg).astype(BF)
    send_all(SGS)
    t_in[x * rings + ring] = t_own[x * rings + ring]
    hid_own[...] = (z * s).astype(BF)
    sg[:, nodes_of(g)] = sg_own[rows_of(g), :]
    hidden[:, nodes_of(g)] = hid_own[rows_of(g), :]

    send_all(HIDS)
    wait_all(SGS)

    for off in range(BAND - 1, -1, -1):

        value = jnp.dot(
            sg[...], adj[:, pl.ds(off * rows, rows)], preferred_element_type=F32
        )
        if off > 0:
            part[off - 1] = value.astype(BF)
        else:
            grad_feats[...] = value + sg[...].astype(F32)

        if off > 0:
            back_copy(off).start()
        if off == 3:
            wait_all(RSUM)
            total = t_in[0].astype(F32)
            for q in range(1, xs * rings):
                total = total + t_in[q].astype(F32)
            for h in range(ZHI):
                u_own[h] = total[h * chunk : h * chunk + chunk]
            send_all(ZSUM)
            u_in[span] = u_own[z_hi]

    wait_all(ZSUM)
    total = u_in[0]
    for q in range(1, ZHI * spans):
        total = total + u_in[q]
    v_own[...] = total * (rows * blocks) ** (-0.5)
    send_all(RALL)
    v_in[ring] = v_own[...]
    for off in range(1, BAND):
        back_copy(off).wait_recv()
    carried = arrived[0].astype(F32)
    for off in range(2, BAND):
        carried = carried + arrived[off - 1].astype(F32)
    grad_feats[...] = root[...] * (grad_feats[...] + carried)
    wait_all(HIDS)
    wait_all(RALL)
    for q in range(rings):
        grad_weight[
            (q // 2) * chunk : (q // 2 + 1) * chunk, (q % 2) * 128 : (q % 2) * 128 + 128
        ] = v_in[q]
    for phase in plans:
        sent_all(phase)
    for off in range(1, BAND):
        halo_copy(off).wait_send()
        back_copy(off).wait_send()


def settle(*refs):
    sems = refs[6]
    copies = [pltpu.make_async_copy(refs[i], refs[3 + i], sems.at[i]) for i in range(3)]
    for copy in copies:
        copy.start()
    for copy in copies:
        copy.wait()


def body(rings, feats, weight, nbr, mult, cotan):
    feat, rows = feats.shape
    slots = nbr.shape[0]
    blocks = lax.axis_size("blk")
    groups = lax.axis_size("grp")
    width = feat * groups
    slice_n = rows // groups
    chunk = feat // (rings // 2)
    spans = blocks // rings
    vmem = pltpu.VMEM
    edges = 256
    most = max(groups, rings * groups // ZHI, ZHI * spans)
    outs = pl.pallas_call(
            functools.partial(kernel, (blocks, groups, rings)),
            out_shape=(
                vmem((feat, rows), BF),
                vmem((feat, rows), F32),
                vmem((feat, width), F32),
            ),
            in_specs=[
                pl.BlockSpec(memory_space=pl.ANY if i in (0, 1, 4) else vmem) for i in range(5)
            ],
            out_specs=(pl.BlockSpec(memory_space=vmem),) * 3,
            scratch_shapes=[
                vmem((slots * 8, 128), jnp.int32),
                vmem((2, slots * 8, 128), BF),
                vmem((edges // 2, 128), jnp.int32),
                vmem((2, edges // 2, 128), BF),
                vmem((width, slice_n), BF),
                vmem((feat, BAND * rows), BF),
                vmem((feat, rows), BF),
                vmem((width, slice_n), BF),
                vmem((width, slice_n), BF),
                vmem((feat, rows), BF),
                vmem((width, slice_n), BF),
                vmem((rows, BAND * rows), BF),
                vmem((16 * 128, edges), BF),
                vmem((128, edges), F32),
                vmem((128, edges), F32),
                vmem((128, edges), F32),
                vmem((128, edges), F32),
                vmem((1, rows), F32),
                vmem((width, width), BF),
                vmem((BAND - 1, feat, rows), BF),
                vmem((BAND - 1, feat, rows), BF),
                vmem((rings * groups // ZHI, ZHI * chunk, 128), BF),
                vmem((rings * groups // ZHI, ZHI * chunk, 128), BF),
                vmem((ZHI, chunk, 128), F32),
                vmem((ZHI * spans, chunk, 128), F32),
                vmem((chunk, 128), F32),
                vmem((rings, chunk, 128), F32),
                pltpu.SemaphoreType.DMA((9, most)),
                pltpu.SemaphoreType.DMA((9, most)),
                pltpu.SemaphoreType.DMA((2, BAND - 1)),
                pltpu.SemaphoreType.DMA((2, BAND - 1)),
                vmem((feat, rows), BF),
                vmem((width, width), BF),
                vmem((feat, rows), BF),
                pltpu.SemaphoreType.DMA((3,)),
            ],
            compiler_params=pltpu.CompilerParams(
                collective_id=0, has_side_effects=True, vmem_limit_bytes=60 * 1024 * 1024
            ),
        )(feats, weight, nbr, mult, cotan)
    return tuple(
        pl.pallas_call(
            settle,
            out_shape=[jax.ShapeDtypeStruct(o.shape, o.dtype) for o in outs],
            in_specs=[pl.BlockSpec(memory_space=vmem)] * 3,
            out_specs=[pl.BlockSpec(memory_space=pl.ANY)] * 3,
            scratch_shapes=[pltpu.SemaphoreType.DMA((3,))],
            compiler_params=pltpu.CompilerParams(vmem_limit_bytes=1024 * 1024),
        )(*outs)
    )


def solution(mesh, rings=RINGS):
    return jax.shard_map(
        functools.partial(body, rings),
        mesh=mesh,
        in_specs=(P("grp", "blk"), P(), P("grp", "blk"), P("grp", "blk"), P("grp", "blk")),
        out_specs=(P("grp", "blk"), P("grp", "blk"), P("grp", None)),
        check_vma=False,
    )
```

```python
import functools

import jax
import jax.numpy as jnp
from jax import lax
from jax.experimental import pallas as pl
from jax.experimental.pallas import tpu as pltpu
from jax.sharding import PartitionSpec as P

BAND = 4
CORES = 2
RINGS = 8
BF = jnp.bfloat16
F32 = jnp.float32
MESH = pl.DeviceIdType.MESH
NT = (((1,), (1,)), ((), ()))
WORDS, MULTS, COTS, AGGS, SGS, HIDS, RSUM, ZSUM, RALL = range(9)
ZHI = 2
PLANE = 16
HI = 16


def kernel(
    shape,
    feats_in,
    weight_in,
    nbr,
    mult,
    cotan_in,
    hidden,
    grad_feats,
    grad_weight,
    words,
    mults,
    gw,
    gm,
    cot_all,
    halo,
    agg_own,
    agg_all,
    sg_own,
    sg,
    hid_own,
    adj,
    spread,
    e_lq,
    e_lr,
    e_hi,
    e_m,
    root,
    w_t,
    part,
    arrived,
    t_own,
    t_in,
    u_own,
    u_in,
    v_own,
    v_in,
    send_sem,
    recv_sem,
    hsend,
    hrecv,
    feats,
    weight,
    cotan,
    load_sem,
):
    blocks, groups, rings = shape
    feat, rows = feats.shape
    width = feat * groups
    slice_n = rows // groups
    spans = blocks // rings
    edge_rows = words.shape[0]
    b = lax.axis_index("blk")
    g = lax.axis_index("grp")
    core = lax.rem(b, CORES)
    ring = lax.rem(b // CORES, rings)
    z_lo = b // (CORES * rings)
    xs = groups // ZHI
    z_hi = g // xs
    x = lax.rem(g, xs)
    span = (z_hi * spans + z_lo * CORES + core)

    def grp_dev(q):
        return (b, q)

    def ring_dev(q):
        return ((z_lo * rings + q) * CORES + core, g)

    def plane_dev(q):
        return (
            (z_lo * rings + lax.rem(q, rings)) * CORES + core,
            z_hi * xs + q // rings,
        )

    def span_dev(q):
        low = lax.rem(q, spans)
        return (
            ((low // CORES) * rings + ring) * CORES + lax.rem(low, CORES),
            (q // spans) * xs + x,
        )

    def rows_of(q):
        return pl.ds(pl.multiple_of(q * feat, feat), feat)

    def nodes_of(q):
        return pl.ds(pl.multiple_of(q * slice_n, slice_n), slice_n)

    def edges_of(q):
        return pl.ds(pl.multiple_of(q * edge_rows, 16), edge_rows)

    plans = {
        WORDS: (grp_dev, g, groups, lambda q: words, lambda q: gw.at[edges_of(q), :]),
        MULTS: (grp_dev, g, groups, lambda q: mults, lambda q: gm.at[:, edges_of(q), :]),
        COTS: (grp_dev, g, groups, lambda q: cotan.at[:, nodes_of(q)], lambda q: cot_all.at[rows_of(q), :]),
        AGGS: (grp_dev, g, groups, lambda q: agg_own.at[:, nodes_of(q)], lambda q: agg_all.at[rows_of(q), :]),
        SGS: (grp_dev, g, groups, lambda q: sg_own.at[rows_of(q), :], lambda q: sg.at[:, nodes_of(q)]),
        HIDS: (grp_dev, g, groups, lambda q: hid_own.at[rows_of(q), :], lambda q: hidden.at[:, nodes_of(q)]),
        RSUM: (plane_dev, x * rings + ring, xs * rings, lambda q: t_own.at[q], lambda q: t_in.at[q]),
        ZSUM: (span_dev, span, ZHI * spans, lambda q: u_own.at[q // spans], lambda q: u_in.at[q]),
        RALL: (ring_dev, ring, rings, lambda q: v_own, lambda q: v_in.at[q]),
    }

    def out_copy(phase, q):
        dev, me, _, src, dst = plans[phase]
        return pltpu.make_async_remote_copy(
            src_ref=src(q),
            dst_ref=dst(me),
            send_sem=send_sem.at[phase, q],
            recv_sem=recv_sem.at[phase, me],
            device_id=dev(q),
            device_id_type=MESH,
        )

    def in_copy(phase, q):
        dev, me, _, src, dst = plans[phase]
        return pltpu.make_async_remote_copy(
            src_ref=src(q),
            dst_ref=dst(q),
            send_sem=send_sem.at[phase, q],
            recv_sem=recv_sem.at[phase, q],
            device_id=dev(q),
            device_id_type=MESH,
        )

    def each(phase, act):
        me, count = plans[phase][1], plans[phase][2]

        @pl.loop(1, count)
        def _(i):
            act(lax.rem(me + i, count))

    def send_all(phase):
        each(phase, lambda q: out_copy(phase, q).start())

    def wait_all(phase):
        each(phase, lambda q: in_copy(phase, q).wait_recv())

    def sent_all(phase):
        each(phase, lambda q: out_copy(phase, q).wait_send())

    def halo_copy(off):
        return pltpu.make_async_remote_copy(
            src_ref=halo.at[:, pl.ds(0, rows)],
            dst_ref=halo.at[:, pl.ds(off * rows, rows)],
            send_sem=hsend.at[0, off - 1],
            recv_sem=hrecv.at[0, off - 1],
            device_id=(lax.rem(b + off, blocks), g),
            device_id_type=MESH,
        )

    def back_copy(off):
        return pltpu.make_async_remote_copy(
            src_ref=part.at[off - 1],
            dst_ref=arrived.at[off - 1],
            send_sem=hsend.at[1, off - 1],
            recv_sem=hrecv.at[1, off - 1],
            device_id=(lax.rem(b - off + blocks, blocks), g),
            device_id_type=MESH,
        )

    loads = [
        pltpu.make_async_copy(here, there, load_sem.at[i])
        for i, (here, there) in enumerate(
            ((feats_in, feats), (weight_in, weight), (cotan_in, cotan))
        )
    ]
    for load in loads:
        load.start()
    barrier = pltpu.get_barrier_semaphore()

    def greet(dev):
        pl.semaphore_signal(barrier, inc=1, device_id=dev, device_id_type=MESH)

    for phase in (WORDS, RSUM, ZSUM):
        each(phase, lambda q, dev=plans[phase][0]: greet(dev(q)))
    for off in range(1, BAND):
        greet((lax.rem(b + off, blocks), g))
        greet((lax.rem(b - off + blocks, blocks), g))

    pairs = nbr.shape[0] // 2
    shift = rows.bit_length() - 1
    code = nbr[...]
    code = (((b - (code >> shift)) & (blocks - 1)) << shift) + (code & (rows - 1))
    amounts = mult[...].astype(F32)

    def plane(value, k):
        return jnp.concatenate(
            [value[k : k + 1, c * 128 : c * 128 + 128] for c in range(PLANE)], axis=0
        )

    for p in range(pairs):
        at = pl.ds(p * PLANE, PLANE)
        words[at, :] = plane(code, 2 * p) + (plane(code, 2 * p + 1) << 16)
        for h in range(2):
            mults[h, at, :] = plane(amounts, 2 * p + h).astype(BF)
    for load in loads:
        load.wait()
    pl.semaphore_wait(
        barrier, groups - 1 + xs * rings - 1 + ZHI * spans - 1 + 2 * (BAND - 1)
    )

    send_all(WORDS)
    send_all(MULTS)
    gw[edges_of(g), :] = words[...]
    gm[:, edges_of(g), :] = mults[...]
    cot_all[rows_of(g), :] = cotan[:, nodes_of(g)]
    w_t[...] = weight[...].astype(F32).T.astype(BF)
    edges = 256
    lane_e = lax.broadcasted_iota(jnp.int32, (128, edges), 1)
    row_l = lax.broadcasted_iota(jnp.int32, (128, edges), 0)
    folds = (lane_e & 15) == (row_l & 15)
    for k in range(16):
        spread[k * 128 : k * 128 + 128, :] = jnp.where(
            folds & ((lane_e >> 4) == k), 1.0, 0.0
        ).astype(BF)
    wait_all(MULTS)

    planes = gw.shape[0] // PLANE
    line = jnp.zeros((PLANE, 128), F32)
    for h in range(2):
        for q in range(planes):
            line = line + gm[h, q * PLANE : q * PLANE + PLANE, :].astype(F32)
    line = lax.rsqrt(1.0 + line)
    for c in range(PLANE):
        root[:, c * 128 : c * 128 + 128] = line[c : c + 1, :]
    halo[:, pl.ds(0, rows)] = (feats[...].astype(F32) * root[...]).astype(BF)
    for off in range(1, BAND):
        halo_copy(off).start()
    send_all(COTS)
    wait_all(WORDS)

    seat = (
        lax.broadcasted_iota(jnp.int32, (PLANE, 8, 128), 2) >> 4
    ) == lax.broadcasted_iota(jnp.int32, (PLANE, 8, 128), 1)

    def seated(value):
        wide = jnp.broadcast_to(value.astype(F32)[:, None, :], (PLANE, 8, 128))
        return jnp.where(seat, wide, 0.0).reshape(PLANE * 8, 128).astype(BF)

    def table(pick):
        wide = jnp.concatenate(
            [seated(pick(h, pl.ds(q * PLANE, PLANE))) for h in range(2) for q in range(planes)],
            axis=1,
        )
        return jnp.dot(wide, spread[...], preferred_element_type=F32)

    def field(low, mask):
        return lambda h, at: (gw[at, :] >> (16 * h + low)) & mask

    e_lr[...] = table(field(0, 15))
    e_lq[...] = table(field(4, 31))
    e_hi[...] = table(field(9, 15))
    e_m[...] = table(lambda h, at: gm[h, at, :])

    lo_chunks = BAND * rows // HI // 16
    sub = lax.broadcasted_iota(jnp.int32, (16, edges), 0)
    own_lane = (lax.broadcasted_iota(jnp.int32, (16, edges), 1) & 15) == sub
    sub_f = sub.astype(F32)
    zero = jnp.zeros((16, edges), BF)
    ones = jnp.ones((16, edges), BF)

    @pl.loop(0, rows // 16, unroll=16)
    def _(t):
        one = pl.ds(t, 1)

        def row(ref):
            return jnp.broadcast_to(ref[one, :], (16, edges))

        low = jnp.where(row(e_lr) == sub_f, row(e_lq), -1.0).astype(BF)
        high = row(e_hi).astype(BF)
        amount = jnp.where(own_lane, row(e_m), 0.0).astype(BF)
        right = jnp.concatenate(
            [jnp.where(low == jnp.asarray(float(c), BF), ones, zero) for c in range(lo_chunks)],
            axis=0,
        )
        left = jnp.concatenate(
            [jnp.where(high == jnp.asarray(float(c), BF), amount, zero) for c in range(HI)],
            axis=0,
        )
        made = lax.dot_general(left, right, NT, preferred_element_type=F32).astype(BF)
        adj[pl.ds(pl.multiple_of(t * 16, 16), 16), :] = jnp.concatenate(
            [made[c * 16 : c * 16 + 16, :] for c in range(HI)], axis=1
        )

    for off in range(1, BAND):
        halo_copy(off).wait_recv()

    step_n = 256

    def forward(q):
        @pl.loop(0, slice_n // step_n)
        def _(i):
            at = pl.ds(pl.multiple_of(q * slice_n + i * step_n, step_n), step_n)
            total = halo[:, at].astype(F32) + lax.dot_general(
                halo[...], adj[at, :], NT, preferred_element_type=F32
            )
            agg_own[:, at] = (root[:, at] * total).astype(BF)

    def forward_send(q):
        forward(q)
        out_copy(AGGS, q).start()

    each(AGGS, forward_send)
    forward(g)
    agg_all[rows_of(g), :] = agg_own[:, nodes_of(g)]
    wait_all(AGGS)
    wait_all(COTS)

    z = jnp.dot(w_t[...], agg_all[...], preferred_element_type=F32)
    s = 1.0 / (1.0 + jnp.exp(-z))
    grad_z = (cot_all[...].astype(F32) * s * (1.0 + z * (1.0 - s))).astype(BF)
    grad_agg = jnp.dot(weight[...], grad_z, preferred_element_type=F32)
    sg_own[...] = (root[:, nodes_of(g)] * grad_agg).astype(BF)
    send_all(SGS)
    product = lax.dot_general(agg_all[...], grad_z, NT, preferred_element_type=F32)
    chunk = feat // (rings // 2)
    for q in range(xs * rings):
        for h in range(ZHI):
            top = (h * xs + q // rings) * feat + (q % rings // 2) * chunk
            t_own[q, h * chunk : h * chunk + chunk, :] = product[
                top : top + chunk, (q % 2) * 128 : (q % 2) * 128 + 128
            ].astype(BF)
    send_all(RSUM)
    t_in[x * rings + ring] = t_own[x * rings + ring]
    hid_own[...] = (z * s).astype(BF)
    sg[:, nodes_of(g)] = sg_own[rows_of(g), :]
    hidden[:, nodes_of(g)] = hid_own[rows_of(g), :]

    send_all(HIDS)
    wait_all(SGS)

    for off in range(BAND - 1, -1, -1):

        value = jnp.dot(
            sg[...], adj[:, pl.ds(off * rows, rows)], preferred_element_type=F32
        )
        if off > 0:
            part[off - 1] = value.astype(BF)
        else:
            grad_feats[...] = value + sg[...].astype(F32)

        if off > 0:
            back_copy(off).start()
        if off == 2:
            wait_all(RSUM)
            total = t_in[0].astype(F32)
            for q in range(1, xs * rings):
                total = total + t_in[q].astype(F32)
            for h in range(ZHI):
                u_own[h] = total[h * chunk : h * chunk + chunk]
            send_all(ZSUM)
            u_in[span] = u_own[z_hi]

    wait_all(ZSUM)
    total = u_in[0]
    for q in range(1, ZHI * spans):
        total = total + u_in[q]
    v_own[...] = total * (rows * blocks) ** (-0.5)
    send_all(RALL)
    v_in[ring] = v_own[...]
    for off in range(1, BAND):
        back_copy(off).wait_recv()
    carried = arrived[0].astype(F32)
    for off in range(2, BAND):
        carried = carried + arrived[off - 1].astype(F32)
    grad_feats[...] = root[...] * (grad_feats[...] + carried)
    wait_all(HIDS)
    wait_all(RALL)
    for q in range(rings):
        grad_weight[
            (q // 2) * chunk : (q // 2 + 1) * chunk, (q % 2) * 128 : (q % 2) * 128 + 128
        ] = v_in[q]
    for phase in plans:
        sent_all(phase)
    for off in range(1, BAND):
        halo_copy(off).wait_send()
        back_copy(off).wait_send()


def settle(*refs):
    sems = refs[6]
    copies = [pltpu.make_async_copy(refs[i], refs[3 + i], sems.at[i]) for i in range(3)]
    for copy in copies:
        copy.start()
    for copy in copies:
        copy.wait()


def body(rings, feats, weight, nbr, mult, cotan):
    feat, rows = feats.shape
    slots = nbr.shape[0]
    blocks = lax.axis_size("blk")
    groups = lax.axis_size("grp")
    width = feat * groups
    slice_n = rows // groups
    chunk = feat // (rings // 2)
    spans = blocks // rings
    vmem = pltpu.VMEM
    edges = 256
    most = max(groups, rings * groups // ZHI, ZHI * spans)
    outs = pl.pallas_call(
            functools.partial(kernel, (blocks, groups, rings)),
            out_shape=(
                vmem((feat, rows), BF),
                vmem((feat, rows), F32),
                vmem((feat, width), F32),
            ),
            in_specs=[
                pl.BlockSpec(memory_space=pl.ANY if i in (0, 1, 4) else vmem) for i in range(5)
            ],
            out_specs=(pl.BlockSpec(memory_space=vmem),) * 3,
            scratch_shapes=[
                vmem((slots * 8, 128), jnp.int32),
                vmem((2, slots * 8, 128), BF),
                vmem((edges // 2, 128), jnp.int32),
                vmem((2, edges // 2, 128), BF),
                vmem((width, slice_n), BF),
                vmem((feat, BAND * rows), BF),
                vmem((feat, rows), BF),
                vmem((width, slice_n), BF),
                vmem((width, slice_n), BF),
                vmem((feat, rows), BF),
                vmem((width, slice_n), BF),
                vmem((rows, BAND * rows), BF),
                vmem((16 * 128, edges), BF),
                vmem((128, edges), F32),
                vmem((128, edges), F32),
                vmem((128, edges), F32),
                vmem((128, edges), F32),
                vmem((1, rows), F32),
                vmem((width, width), BF),
                vmem((BAND - 1, feat, rows), BF),
                vmem((BAND - 1, feat, rows), BF),
                vmem((rings * groups // ZHI, ZHI * chunk, 128), BF),
                vmem((rings * groups // ZHI, ZHI * chunk, 128), BF),
                vmem((ZHI, chunk, 128), F32),
                vmem((ZHI * spans, chunk, 128), F32),
                vmem((chunk, 128), F32),
                vmem((rings, chunk, 128), F32),
                pltpu.SemaphoreType.DMA((9, most)),
                pltpu.SemaphoreType.DMA((9, most)),
                pltpu.SemaphoreType.DMA((2, BAND - 1)),
                pltpu.SemaphoreType.DMA((2, BAND - 1)),
                vmem((feat, rows), BF),
                vmem((width, width), BF),
                vmem((feat, rows), BF),
                pltpu.SemaphoreType.DMA((3,)),
            ],
            compiler_params=pltpu.CompilerParams(
                collective_id=0, has_side_effects=True, vmem_limit_bytes=60 * 1024 * 1024
            ),
        )(feats, weight, nbr, mult, cotan)
    return tuple(
        pl.pallas_call(
            settle,
            out_shape=[jax.ShapeDtypeStruct(o.shape, o.dtype) for o in outs],
            in_specs=[pl.BlockSpec(memory_space=vmem)] * 3,
            out_specs=[pl.BlockSpec(memory_space=pl.ANY)] * 3,
            scratch_shapes=[pltpu.SemaphoreType.DMA((3,))],
            compiler_params=pltpu.CompilerParams(vmem_limit_bytes=1024 * 1024),
        )(*outs)
    )


def solution(mesh, rings=RINGS):
    return jax.shard_map(
        functools.partial(body, rings),
        mesh=mesh,
        in_specs=(P("grp", "blk"), P(), P("grp", "blk"), P("grp", "blk"), P("grp", "blk")),
        out_specs=(P("grp", "blk"), P("grp", "blk"), P("grp", None)),
        check_vma=False,
    )
```

```python
import functools

import jax
import jax.numpy as jnp
from jax import lax
from jax.experimental import pallas as pl
from jax.experimental.pallas import tpu as pltpu
from jax.sharding import PartitionSpec as P

BAND = 4
CORES = 2
RINGS = 8
BF = jnp.bfloat16
F32 = jnp.float32
MESH = pl.DeviceIdType.MESH
NT = (((1,), (1,)), ((), ()))
WORDS, MULTS, COTS, AGGS, SGS, HIDS, XSUM, RSUM, ZSUM, RALL = range(10)
ZHI = 2
PLANE = 16
HI = 16


def kernel(
    shape,
    feats_in,
    weight_in,
    nbr,
    mult,
    cotan_in,
    hidden,
    grad_feats,
    grad_weight,
    words,
    mults,
    gw,
    gm,
    cot_all,
    halo,
    agg_own,
    agg_all,
    sg_own,
    sg,
    hid_own,
    adj,
    spread,
    e_lq,
    e_lr,
    e_hi,
    e_m,
    root,
    w_t,
    part,
    arrived,
    gw_own,
    gw_in,
    t_own,
    t_in,
    u_own,
    u_in,
    v_own,
    v_in,
    send_sem,
    recv_sem,
    hsend,
    hrecv,
    feats,
    weight,
    cotan,
    load_sem,
):
    blocks, groups, rings = shape
    feat, rows = feats.shape
    width = feat * groups
    slice_n = rows // groups
    spans = blocks // rings
    edge_rows = words.shape[0]
    b = lax.axis_index("blk")
    g = lax.axis_index("grp")
    core = lax.rem(b, CORES)
    ring = lax.rem(b // CORES, rings)
    z_lo = b // (CORES * rings)
    xs = groups // ZHI
    z_hi = g // xs
    x = lax.rem(g, xs)
    span = (z_hi * spans + z_lo * CORES + core)

    def grp_dev(q):
        return (b, q)

    def ring_dev(q):
        return ((z_lo * rings + q) * CORES + core, g)

    def x_dev(q):
        return (b, z_hi * xs + q)

    def span_dev(q):
        low = lax.rem(q, spans)
        return (
            ((low // CORES) * rings + ring) * CORES + lax.rem(low, CORES),
            (q // spans) * xs + x,
        )

    def rows_of(q):
        return pl.ds(pl.multiple_of(q * feat, feat), feat)

    def nodes_of(q):
        return pl.ds(pl.multiple_of(q * slice_n, slice_n), slice_n)

    def edges_of(q):
        return pl.ds(pl.multiple_of(q * edge_rows, 16), edge_rows)

    plans = {
        WORDS: (grp_dev, g, groups, lambda q: words, lambda q: gw.at[edges_of(q), :]),
        MULTS: (grp_dev, g, groups, lambda q: mults, lambda q: gm.at[:, edges_of(q), :]),
        COTS: (grp_dev, g, groups, lambda q: cotan.at[:, nodes_of(q)], lambda q: cot_all.at[rows_of(q), :]),
        AGGS: (grp_dev, g, groups, lambda q: agg_own.at[:, nodes_of(q)], lambda q: agg_all.at[rows_of(q), :]),
        SGS: (grp_dev, g, groups, lambda q: sg_own.at[rows_of(q), :], lambda q: sg.at[:, nodes_of(q)]),
        HIDS: (grp_dev, g, groups, lambda q: hid_own.at[rows_of(q), :], lambda q: hidden.at[:, nodes_of(q)]),
        XSUM: (x_dev, x, xs, lambda q: gw_own.at[:, q], lambda q: gw_in.at[q]),
        RSUM: (ring_dev, ring, rings, lambda q: t_own.at[q], lambda q: t_in.at[q]),
        ZSUM: (span_dev, span, ZHI * spans, lambda q: u_own.at[q // spans], lambda q: u_in.at[q]),
        RALL: (ring_dev, ring, rings, lambda q: v_own, lambda q: v_in.at[q]),
    }

    def out_copy(phase, q):
        dev, me, _, src, dst = plans[phase]
        return pltpu.make_async_remote_copy(
            src_ref=src(q),
            dst_ref=dst(me),
            send_sem=send_sem.at[phase, q],
            recv_sem=recv_sem.at[phase, me],
            device_id=dev(q),
            device_id_type=MESH,
        )

    def in_copy(phase, q):
        dev, me, _, src, dst = plans[phase]
        return pltpu.make_async_remote_copy(
            src_ref=src(q),
            dst_ref=dst(q),
            send_sem=send_sem.at[phase, q],
            recv_sem=recv_sem.at[phase, q],
            device_id=dev(q),
            device_id_type=MESH,
        )

    def each(phase, act):
        me, count = plans[phase][1], plans[phase][2]

        @pl.loop(1, count)
        def _(i):
            act(lax.rem(me + i, count))

    def send_all(phase):
        each(phase, lambda q: out_copy(phase, q).start())

    def wait_all(phase):
        each(phase, lambda q: in_copy(phase, q).wait_recv())

    def sent_all(phase):
        each(phase, lambda q: out_copy(phase, q).wait_send())

    def halo_copy(off):
        return pltpu.make_async_remote_copy(
            src_ref=halo.at[:, pl.ds(0, rows)],
            dst_ref=halo.at[:, pl.ds(off * rows, rows)],
            send_sem=hsend.at[0, off - 1],
            recv_sem=hrecv.at[0, off - 1],
            device_id=(lax.rem(b + off, blocks), g),
            device_id_type=MESH,
        )

    def back_copy(off):
        return pltpu.make_async_remote_copy(
            src_ref=part.at[off - 1],
            dst_ref=arrived.at[off - 1],
            send_sem=hsend.at[1, off - 1],
            recv_sem=hrecv.at[1, off - 1],
            device_id=(lax.rem(b - off + blocks, blocks), g),
            device_id_type=MESH,
        )

    loads = [
        pltpu.make_async_copy(here, there, load_sem.at[i])
        for i, (here, there) in enumerate(
            ((feats_in, feats), (weight_in, weight), (cotan_in, cotan))
        )
    ]
    for load in loads:
        load.start()
    barrier = pltpu.get_barrier_semaphore()

    def greet(dev):
        pl.semaphore_signal(barrier, inc=1, device_id=dev, device_id_type=MESH)

    for phase in (WORDS, RSUM, ZSUM):
        each(phase, lambda q, dev=plans[phase][0]: greet(dev(q)))
    for off in range(1, BAND):
        greet((lax.rem(b + off, blocks), g))
        greet((lax.rem(b - off + blocks, blocks), g))

    pairs = nbr.shape[0] // 2
    shift = rows.bit_length() - 1
    code = nbr[...]
    code = (((b - (code >> shift)) & (blocks - 1)) << shift) + (code & (rows - 1))
    amounts = mult[...].astype(F32)

    def plane(value, k):
        return jnp.concatenate(
            [value[k : k + 1, c * 128 : c * 128 + 128] for c in range(PLANE)], axis=0
        )

    for p in range(pairs):
        at = pl.ds(p * PLANE, PLANE)
        words[at, :] = plane(code, 2 * p) + (plane(code, 2 * p + 1) << 16)
        for h in range(2):
            mults[h, at, :] = plane(amounts, 2 * p + h).astype(BF)
    for load in loads:
        load.wait()
    pl.semaphore_wait(
        barrier, groups - 1 + rings - 1 + ZHI * spans - 1 + 2 * (BAND - 1)
    )

    send_all(WORDS)
    send_all(MULTS)
    gw[edges_of(g), :] = words[...]
    gm[:, edges_of(g), :] = mults[...]
    cot_all[rows_of(g), :] = cotan[:, nodes_of(g)]
    w_t[...] = weight[...].astype(F32).T.astype(BF)
    edges = 256
    lane_e = lax.broadcasted_iota(jnp.int32, (128, edges), 1)
    row_l = lax.broadcasted_iota(jnp.int32, (128, edges), 0)
    folds = (lane_e & 15) == (row_l & 15)
    for k in range(16):
        spread[k * 128 : k * 128 + 128, :] = jnp.where(
            folds & ((lane_e >> 4) == k), 1.0, 0.0
        ).astype(BF)
    wait_all(MULTS)

    planes = gw.shape[0] // PLANE
    line = jnp.zeros((PLANE, 128), F32)
    for h in range(2):
        for q in range(planes):
            line = line + gm[h, q * PLANE : q * PLANE + PLANE, :].astype(F32)
    line = lax.rsqrt(1.0 + line)
    for c in range(PLANE):
        root[:, c * 128 : c * 128 + 128] = line[c : c + 1, :]
    halo[:, pl.ds(0, rows)] = (feats[...].astype(F32) * root[...]).astype(BF)
    for off in range(1, BAND):
        halo_copy(off).start()
    send_all(COTS)
    wait_all(WORDS)

    seat = (
        lax.broadcasted_iota(jnp.int32, (PLANE, 8, 128), 2) >> 4
    ) == lax.broadcasted_iota(jnp.int32, (PLANE, 8, 128), 1)

    def seated(value):
        wide = jnp.broadcast_to(value.astype(F32)[:, None, :], (PLANE, 8, 128))
        return jnp.where(seat, wide, 0.0).reshape(PLANE * 8, 128).astype(BF)

    def table(pick):
        wide = jnp.concatenate(
            [seated(pick(h, pl.ds(q * PLANE, PLANE))) for h in range(2) for q in range(planes)],
            axis=1,
        )
        return jnp.dot(wide, spread[...], preferred_element_type=F32)

    def field(low, mask):
        return lambda h, at: (gw[at, :] >> (16 * h + low)) & mask

    e_lr[...] = table(field(0, 15))
    e_lq[...] = table(field(4, 31))
    e_hi[...] = table(field(9, 15))
    e_m[...] = table(lambda h, at: gm[h, at, :])

    lo_chunks = BAND * rows // HI // 16
    sub = lax.broadcasted_iota(jnp.int32, (16, edges), 0)
    own_lane = (lax.broadcasted_iota(jnp.int32, (16, edges), 1) & 15) == sub
    sub_f = sub.astype(F32)
    zero = jnp.zeros((16, edges), BF)
    ones = jnp.ones((16, edges), BF)

    @pl.loop(0, rows // 16, unroll=8)
    def _(t):
        one = pl.ds(t, 1)

        def row(ref):
            return jnp.broadcast_to(ref[one, :], (16, edges))

        low = jnp.where(row(e_lr) == sub_f, row(e_lq), -1.0).astype(BF)
        high = row(e_hi).astype(BF)
        amount = jnp.where(own_lane, row(e_m), 0.0).astype(BF)
        right = jnp.concatenate(
            [jnp.where(low == jnp.asarray(float(c), BF), ones, zero) for c in range(lo_chunks)],
            axis=0,
        )
        left = jnp.concatenate(
            [jnp.where(high == jnp.asarray(float(c), BF), amount, zero) for c in range(HI)],
            axis=0,
        )
        made = lax.dot_general(left, right, NT, preferred_element_type=F32).astype(BF)
        adj[pl.ds(pl.multiple_of(t * 16, 16), 16), :] = jnp.concatenate(
            [made[c * 16 : c * 16 + 16, :] for c in range(HI)], axis=1
        )

    for off in range(1, BAND):
        halo_copy(off).wait_recv()

    step_n = 256

    def forward(q):
        @pl.loop(0, slice_n // step_n)
        def _(i):
            at = pl.ds(pl.multiple_of(q * slice_n + i * step_n, step_n), step_n)
            total = halo[:, at].astype(F32) + lax.dot_general(
                halo[...], adj[at, :], NT, preferred_element_type=F32
            )
            agg_own[:, at] = (root[:, at] * total).astype(BF)

    def forward_send(q):
        forward(q)
        out_copy(AGGS, q).start()

    each(AGGS, forward_send)
    forward(g)
    agg_all[rows_of(g), :] = agg_own[:, nodes_of(g)]
    wait_all(AGGS)
    wait_all(COTS)

    z = jnp.dot(w_t[...], agg_all[...], preferred_element_type=F32)
    s = 1.0 / (1.0 + jnp.exp(-z))
    grad_z = (cot_all[...].astype(F32) * s * (1.0 + z * (1.0 - s))).astype(BF)
    grad_agg = jnp.dot(weight[...], grad_z, preferred_element_type=F32)
    sg_own[...] = (root[:, nodes_of(g)] * grad_agg).astype(BF)
    send_all(SGS)
    product = lax.dot_general(agg_all[...], grad_z, NT, preferred_element_type=F32)
    for q in range(groups):
        gw_own[q // xs, q % xs] = product[q * feat : q * feat + feat, :].astype(BF)
    send_all(XSUM)
    hid_own[...] = (z * s).astype(BF)
    sg[:, nodes_of(g)] = sg_own[rows_of(g), :]
    gw_in[x] = gw_own[:, x]
    hidden[:, nodes_of(g)] = hid_own[rows_of(g), :]

    chunk = feat // (rings // 2)
    wait_all(XSUM)
    total = gw_in[0].astype(F32)
    for q in range(1, xs):
        total = total + gw_in[q].astype(F32)
    for q in range(rings):
        t_own[q] = total[
            :, (q // 2) * chunk : (q // 2 + 1) * chunk, (q % 2) * 128 : (q % 2) * 128 + 128
        ]
    send_all(RSUM)
    t_in[ring] = t_own[ring]
    send_all(HIDS)
    wait_all(SGS)

    for off in range(BAND - 1, -1, -1):

        value = jnp.dot(
            sg[...], adj[:, pl.ds(off * rows, rows)], preferred_element_type=F32
        )
        if off > 0:
            part[off - 1] = value.astype(BF)
        else:
            grad_feats[...] = value + sg[...].astype(F32)

        if off > 0:
            back_copy(off).start()
        if off == 2:
            wait_all(RSUM)
            total = t_in[0]
            for q in range(1, rings):
                total = total + t_in[q]
            u_own[...] = total
            send_all(ZSUM)
            u_in[span] = u_own[z_hi]

    wait_all(ZSUM)
    total = u_in[0]
    for q in range(1, ZHI * spans):
        total = total + u_in[q]
    v_own[...] = total * (rows * blocks) ** (-0.5)
    send_all(RALL)
    v_in[ring] = v_own[...]
    for off in range(1, BAND):
        back_copy(off).wait_recv()
    carried = arrived[0].astype(F32)
    for off in range(2, BAND):
        carried = carried + arrived[off - 1].astype(F32)
    grad_feats[...] = root[...] * (grad_feats[...] + carried)
    wait_all(HIDS)
    wait_all(RALL)
    for q in range(rings):
        grad_weight[
            (q // 2) * chunk : (q // 2 + 1) * chunk, (q % 2) * 128 : (q % 2) * 128 + 128
        ] = v_in[q]
    for phase in plans:
        sent_all(phase)
    for off in range(1, BAND):
        halo_copy(off).wait_send()
        back_copy(off).wait_send()


def settle(*refs):
    sems = refs[6]
    copies = [pltpu.make_async_copy(refs[i], refs[3 + i], sems.at[i]) for i in range(3)]
    for copy in copies:
        copy.start()
    for copy in copies:
        copy.wait()


def body(rings, feats, weight, nbr, mult, cotan):
    feat, rows = feats.shape
    slots = nbr.shape[0]
    blocks = lax.axis_size("blk")
    groups = lax.axis_size("grp")
    width = feat * groups
    slice_n = rows // groups
    chunk = feat // (rings // 2)
    spans = blocks // rings
    vmem = pltpu.VMEM
    edges = 256
    most = max(groups, rings, ZHI * spans)
    outs = pl.pallas_call(
            functools.partial(kernel, (blocks, groups, rings)),
            out_shape=(
                vmem((feat, rows), BF),
                vmem((feat, rows), F32),
                vmem((feat, width), F32),
            ),
            in_specs=[
                pl.BlockSpec(memory_space=pl.ANY if i in (0, 1, 4) else vmem) for i in range(5)
            ],
            out_specs=(pl.BlockSpec(memory_space=vmem),) * 3,
            scratch_shapes=[
                vmem((slots * 8, 128), jnp.int32),
                vmem((2, slots * 8, 128), BF),
                vmem((edges // 2, 128), jnp.int32),
                vmem((2, edges // 2, 128), BF),
                vmem((width, slice_n), BF),
                vmem((feat, BAND * rows), BF),
                vmem((feat, rows), BF),
                vmem((width, slice_n), BF),
                vmem((width, slice_n), BF),
                vmem((feat, rows), BF),
                vmem((width, slice_n), BF),
                vmem((rows, BAND * rows), BF),
                vmem((16 * 128, edges), BF),
                vmem((128, edges), F32),
                vmem((128, edges), F32),
                vmem((128, edges), F32),
                vmem((128, edges), F32),
                vmem((1, rows), F32),
                vmem((width, width), BF),
                vmem((BAND - 1, feat, rows), BF),
                vmem((BAND - 1, feat, rows), BF),
                vmem((ZHI, groups // ZHI, feat, width), BF),
                vmem((groups // ZHI, ZHI, feat, width), BF),
                vmem((rings, ZHI, chunk, 128), F32),
                vmem((rings, ZHI, chunk, 128), F32),
                vmem((ZHI, chunk, 128), F32),
                vmem((ZHI * spans, chunk, 128), F32),
                vmem((chunk, 128), F32),
                vmem((rings, chunk, 128), F32),
                pltpu.SemaphoreType.DMA((10, most)),
                pltpu.SemaphoreType.DMA((10, most)),
                pltpu.SemaphoreType.DMA((2, BAND - 1)),
                pltpu.SemaphoreType.DMA((2, BAND - 1)),
                vmem((feat, rows), BF),
                vmem((width, width), BF),
                vmem((feat, rows), BF),
                pltpu.SemaphoreType.DMA((3,)),
            ],
            compiler_params=pltpu.CompilerParams(
                collective_id=0, has_side_effects=True, vmem_limit_bytes=60 * 1024 * 1024
            ),
        )(feats, weight, nbr, mult, cotan)
    return tuple(
        pl.pallas_call(
            settle,
            out_shape=[jax.ShapeDtypeStruct(o.shape, o.dtype) for o in outs],
            in_specs=[pl.BlockSpec(memory_space=vmem)] * 3,
            out_specs=[pl.BlockSpec(memory_space=pl.ANY)] * 3,
            scratch_shapes=[pltpu.SemaphoreType.DMA((3,))],
            compiler_params=pltpu.CompilerParams(vmem_limit_bytes=1024 * 1024),
        )(*outs)
    )


def solution(mesh, rings=RINGS):
    return jax.shard_map(
        functools.partial(body, rings),
        mesh=mesh,
        in_specs=(P("grp", "blk"), P(), P("grp", "blk"), P("grp", "blk"), P("grp", "blk")),
        out_specs=(P("grp", "blk"), P("grp", "blk"), P("grp", None)),
        check_vma=False,
    )
```
